256 devices in a mesh: sec: 2 (over z_hi), grp: 8 (over y, core), rank: 16 (over x, z_lo).
Axes of the slice: x: 4, y: 4, z: 8 (z_hi: 2, z_lo: 4; z = z_hi * 4 + z_lo), core: 2. Of those that a mesh axis runs over, the one named last changes fastest.
Arguments:
- queries: bfloat16 [16, 128, 8192], P(('sec', 'grp')), may hold values from -6 to 14
- kv_cache: bfloat16 [16, 16384, 2048], P(('sec', 'grp'), 'rank'), may hold values from -6 to 10
- key_scale: float32 [1024], replicated, may hold values from 0.5 to 2
- fresh_input: bfloat16 [16, 128, 8192], P(('sec', 'grp'), None, 'rank'), may hold values from -6 to 6
- kv_weight: bfloat16 [8192, 2048], P('rank'), may hold values from -0.0625 to 0.0625
- lengths: int32 [16, 1], P(('sec', 'grp')), may hold values from 1 to 16384
- page_list: int32 [4096], P(('sec', 'grp', 'rank')), may hold values from 0 to 63, as said below
- owners: int32 [4096, 1], P(('sec', 'grp', 'rank')), may hold values from 0 to 15; in each aligned block of 16 rows (0 to 15, 16 to 31, ...) at most 2 rows name the same one
Outputs:
- attended: bfloat16 [16, 128, 8192], P(('sec', 'grp'), None, 'rank')
- handed: bfloat16 [256, 32, 16, 2048], P(('sec', 'grp', 'rank'))
The draws below stay inside these ranges and needn't reach their ends.
Inputs may be any that keep to these rules, and one draw needn't show every extreme that they name: `page_list`: the 16 entries of one device are distinct page numbers of its own cache. `owners`: among the 16 entries of one device at most 2 name the same owner, and some device has exactly 2 for one owner.
All inputs are finite; a program needn't handle non-finite values.
Results may differ from the reference program's by a relative error of at most 0.0045.
The reference program's roundings to bfloat16 on the way (of `fresh_kv`, `query_rot`, `cache_keys`, `fresh_keys` and `rounded`) count: a program that leaves them out, or rounds other values in their place, can miss the bound.
Values may be sent and summed in bfloat16 or wider, within the bound.
A program may use at most 192 MiB of HBM per device.

```python
import math
import jax
import jax.numpy as jnp
import numpy as np
from jax import lax

D = 8192
HEADS = 64
KVH = 8
HD = 128
ROWS = 128
CTX = 1024
PAGE = 16
GQ = 8
KVW = 1024
QW = 8192
PAGES = 64
FIN = 16
CAP = 2
SEQ = 16384
GROUPS = 16
N_GRP = 8
N_RANK = 16


def draw_queries(key, part):
    key = jax.random.fold_in(key, 11)
    key_first = jax.random.fold_in(key, 0)
    base_values = jnp.clip(jax.random.normal(key_first, (GROUPS, ROWS, QW), jnp.float32), -6.0, 6.0)
    return base_values.astype(jnp.bfloat16)


def draw_kv_cache(key, part):
    key = jax.random.fold_in(key, 5)
    key_first = jax.random.fold_in(key, 0)
    base_values = jnp.clip(jax.random.normal(key_first, (GROUPS, SEQ, 2 * KVW), jnp.float32), -6.0, 6.0)
    return base_values.astype(jnp.bfloat16)


def draw_page_list(key, part):
    key = jax.random.fold_in(key, 7)
    device_keys = jax.random.split(key, GROUPS * N_RANK)
    chosen = jax.vmap(lambda device_key: jax.random.permutation(device_key, PAGES)[:FIN])(device_keys)
    return chosen.reshape(GROUPS * N_RANK * FIN).astype(jnp.int32)


def with_ends(array, stream_key, low, high):
    longest = array.shape.index(max(array.shape))
    spots = []
    for shift in (0, 1):
        where = [jax.random.randint(jax.random.fold_in(stream_key, axis), (), 0, length) for axis, length in enumerate(array.shape)]
        where[longest] = (where[longest] + shift) % array.shape[longest]
        spots.append(tuple(where))
    return array.at[spots[0]].set(low).at[spots[1]].set(high)


def block_scale(stream_key, extent, cuts, least, largest):
    def one(dim, parts):
        draws = jax.random.uniform(jax.random.fold_in(jax.random.fold_in(stream_key, 6), dim), (parts,), jnp.float32, least / len(cuts), largest / len(cuts))
        return jnp.repeat(jnp.exp(draws), extent[dim] // parts).reshape((-1,) + (1,) * (len(extent) - dim - 1))

    loudness = one(*cuts[0])
    for cut in cuts[1:]:
        loudness = loudness * one(*cut)
    return loudness


def assign_block(own_key, own, number, rows, count, top, bound, slope):
    sequence = jax.random.permutation(own_key, count)
    heavy_load, ordinary = load_shares(count, rows * top, bound, slope, True), load_shares(count, rows * top, bound, slope, False)
    places = jnp.arange(count)

    def named(sizes, rotation):
        used = int((sizes > 0).sum())
        fixed = max(1, used // 4)
        passed = fixed + (places - fixed + rotation * (used - fixed)) % max(1, count - fixed)
        return jnp.zeros((count,), jnp.int32).at[sequence[jnp.where(places < fixed, places, passed)]].set(jnp.asarray(sizes, jnp.int32))

    sizes = jnp.where(number % 4 == 0, named(heavy_load, number // 4), named(ordinary, number - number // 4 - 1))
    mixed = jax.random.permutation(jax.random.fold_in(own, 3), count)
    giver, taker = mixed[0:count // 2 * 2:2], mixed[1:count // 2 * 2:2]
    slack = jnp.minimum(sizes[giver] - 1, bound - sizes[taker]) // 2
    slack = jnp.where((giver == sequence[0]) | (taker == sequence[0]) | (sizes[taker] == 0), 0, jnp.maximum(slack, 0))
    passed = jax.random.randint(jax.random.fold_in(own, 4), (count // 2,), 0, 1 << 20) % (slack + 1)
    sizes = sizes.at[giver].add(-passed).at[taker].add(passed)
    labels = jnp.searchsorted(jnp.cumsum(sizes), jnp.arange(rows * top), side="right").astype(jnp.int32)
    grid = labels.reshape(top, rows).T
    grid = grid[jax.random.permutation(jax.random.fold_in(own, 1), rows)]
    rotation = jax.random.randint(jax.random.fold_in(own, 2), (rows, 1), 0, top)
    return jnp.take_along_axis(grid, (jnp.arange(top)[None, :] + rotation) % top, axis=1)


def load_shares(number_of, total, bound, slope, full):
    weights = [(1 << 20) // math.isqrt(grade ** slope) + 1 for grade in range(1, number_of + 1)]
    largest = bound if full else min(bound, max(-(-total // number_of), total * weights[0] // sum(weights)))
    least = 1 if total - largest >= number_of - 1 else 0
    given, rest = [largest] + [least] * (number_of - 1), total - largest - least * (number_of - 1)
    while rest > 0:
        movable = [i for i in range(1, number_of) if given[i] < largest] or [i for i in range(1, number_of) if given[i] < bound]
        mass, remaining = sum([weights[i] for i in movable]), rest
        for i in movable:
            more = min(bound - given[i], max(1, remaining * weights[i] // mass), rest)
            given[i] = given[i] + more
            rest = rest - more
    return np.array(given)


def normal_values(own_key, extent, scale, reach, cuts=(), kind=jnp.bfloat16):
    result = jax.random.normal(own_key, extent, jnp.float32) * scale
    if len(cuts) > 0:
        result = block_scale(own_key, extent, cuts, -0.22, 0.18) * result
    return jnp.clip(result, min=-reach, max=reach).astype(kind)


def setup_inputs(seed: int = 0) -> dict:
    keys = jax.random.split(jax.random.key(seed), 9)
    queries = draw_queries(jax.random.fold_in(keys[8], 71), 0)
    kv_cache = draw_kv_cache(jax.random.fold_in(keys[8], 71), 0)
    key_scale = jnp.clip(jnp.exp(jax.random.uniform(keys[2], (KVW,), jnp.float32, math.log(0.5), math.log(2.0))), 0.5, 2.0)
    fresh_input = normal_values(keys[3], (GROUPS, ROWS, D), 1.0, 6.0, ((0, 16), (2, 16)))
    kv_weight = normal_values(keys[4], (D, 2 * KVW), D ** -0.5, 0.0625, ((0, 16),))
    lengths = with_ends(jax.random.randint(keys[5], (GROUPS, 1), 1, SEQ + 1), jax.random.fold_in(keys[5], 1), 1, SEQ).astype(jnp.int32)
    page_list = draw_page_list(jax.random.fold_in(keys[8], 71), 0)
    owners_keys = jax.random.split(jax.random.fold_in(keys[7], 1), (GROUPS * N_RANK * FIN) // FIN)
    owners_turns = jax.random.permutation(jax.random.fold_in(keys[7], 3), (GROUPS * N_RANK * FIN) // FIN)
    owners = jax.vmap(lambda own, number: assign_block(jax.random.fold_in(keys[7], 2), own, number, FIN, N_RANK, 1, CAP, 1))(owners_keys, owners_turns).reshape((GROUPS * N_RANK * FIN, 1))
    return dict(queries=queries, kv_cache=kv_cache, key_scale=key_scale, fresh_input=fresh_input, kv_weight=kv_weight, lengths=lengths, page_list=page_list, owners=owners)


ROPE_BASE = 500000.0
NEG_FILL = -1e+30

def rope_tables(positions):
    half_width = HD // 2
    steps_index = jnp.arange(half_width, dtype=jnp.float32)
    inverse = jnp.exp(steps_index * (-2.0 * math.log(ROPE_BASE) / HD))
    angles = positions.astype(jnp.float32)[:, None] * inverse[None, :]
    return (jnp.cos(angles)[:, None, :], jnp.sin(angles)[:, None, :])

def rotate_heads(values, cosine, sine_part):
    half_width = HD // 2
    first_half = values[..., :half_width]
    second_half = values[..., half_width:]
    return jnp.concatenate([first_half * cosine - second_half * sine_part, second_half * cosine + first_half * sine_part], axis=-1)

def to_half(values):
    return lax.optimization_barrier(values.astype(jnp.bfloat16))

def attend_group(group_item, key_scale, kv_weight):
    query_rows, cache_rows, rows_in, length = group_item
    row_share = ROWS // N_RANK
    row_ids = jnp.arange(ROWS, dtype=jnp.int32)
    positions = length + row_ids
    cosine, sine_part = rope_tables(positions)
    query_rot = to_half(rotate_heads(query_rows.astype(jnp.float32).reshape(ROWS, HEADS, HD), cosine, sine_part))
    fresh_kv = to_half(jnp.dot(rows_in, kv_weight, preferred_element_type=jnp.float32))
    fresh_keys = to_half(rotate_heads(fresh_kv[:, :KVW].astype(jnp.float32).reshape(ROWS, KVH, HD), cosine, sine_part))
    cache_pos = jnp.arange(SEQ, dtype=jnp.int32)
    cache_cos, cache_sin = rope_tables(cache_pos)
    scaled = (cache_rows[:, :KVW].astype(jnp.float32) * key_scale[None, :]).reshape(SEQ, KVH, HD)
    cache_keys = to_half(rotate_heads(scaled, cache_cos, cache_sin))
    keys_all = jnp.concatenate([cache_keys.reshape(N_RANK, CTX, KVH, HD), fresh_keys.reshape(N_RANK, row_share, KVH, HD)], axis=1)
    vals_all = jnp.concatenate([cache_rows[:, KVW:].reshape(N_RANK, CTX, KVH, HD), fresh_kv[:, KVW:].reshape(N_RANK, row_share, KVH, HD)], axis=1)
    cache_ok = jnp.broadcast_to((cache_pos < length).reshape(1, N_RANK, CTX), (ROWS, N_RANK, CTX))
    fresh_ok = (row_ids[None, :] <= row_ids[:, None]).reshape(ROWS, N_RANK, row_share)
    allowed = jnp.concatenate([cache_ok, fresh_ok], axis=2)[:, None]
    query_groups = query_rot.reshape(ROWS, KVH, GQ, HD).transpose(1, 0, 2, 3)

    def per_head(head_item):
        query_head, key_head, value_head = head_item
        scores = jnp.einsum('rgd,nkd->rgnk', query_head.astype(jnp.float32), key_head.astype(jnp.float32)) / math.sqrt(HD)
        masked = jnp.where(allowed, scores, NEG_FILL)
        row_peak = lax.optimization_barrier(jnp.max(masked, axis=-1))
        weights = jnp.where(allowed, jnp.exp(masked - row_peak[..., None]), 0.0)
        row_total = lax.optimization_barrier(jnp.sum(weights, axis=-1))
        rounded = to_half(weights).astype(jnp.float32)
        numerator = jnp.einsum('rgnk,nkd->rgnd', rounded, value_head.astype(jnp.float32))
        row_top = lax.optimization_barrier(jnp.max(row_peak, axis=-1))
        factor = jnp.exp(row_peak - row_top[..., None])
        return lax.optimization_barrier(jnp.sum(numerator * factor[..., None], axis=2)) / lax.optimization_barrier(jnp.sum(row_total * factor, axis=2))[..., None]
    outputs = lax.map(per_head, (query_groups, keys_all.transpose(2, 0, 1, 3), vals_all.transpose(2, 0, 1, 3)))
    return outputs.transpose(1, 0, 2, 3).reshape(ROWS, QW).astype(jnp.bfloat16)

def hand_pages(kv_cache, page_list, owners):
    page_blocks = kv_cache[:N_GRP].reshape(N_GRP, N_RANK, PAGES, PAGE, 2 * KVW)
    listed = page_list.reshape(GROUPS, N_RANK, FIN)[:N_GRP].astype(jnp.int32)
    owner_ids = owners.reshape(GROUPS, N_RANK, FIN)[:N_GRP].astype(jnp.int32)
    targets = jnp.arange(N_RANK, dtype=jnp.int32)
    onehot = (owner_ids[..., None] == targets).astype(jnp.int32)
    running = jnp.cumsum(onehot, axis=2).astype(jnp.int32)
    slot_index = lax.optimization_barrier(jnp.sum(onehot * running, axis=-1)).astype(jnp.int32) - 1
    places = jnp.arange(CAP, dtype=jnp.int32)
    matches = (owner_ids[:, :, None, None, :] == targets[None, None, :, None, None]) & (slot_index[:, :, None, None, :] == places[None, None, None, :, None])
    present = jnp.any(matches, axis=-1)
    chosen = lax.optimization_barrier(jnp.sum(jnp.where(matches, listed[:, :, None, None, :], 0), axis=-1)).astype(jnp.int32)
    group_ids = jnp.arange(N_GRP, dtype=jnp.int32)[:, None, None, None]
    source_ids = jnp.arange(N_RANK, dtype=jnp.int32)[None, :, None, None]
    moved_pages = page_blocks[group_ids, source_ids, chosen]
    moved_pages = jnp.where(present[..., None, None], moved_pages, jnp.zeros((), jnp.bfloat16))
    moved_pages = moved_pages.transpose(0, 2, 1, 3, 4, 5).reshape(N_GRP * N_RANK, N_RANK * CAP, PAGE, 2 * KVW)
    return jnp.concatenate([jnp.zeros_like(moved_pages), moved_pages], axis=0)

def reference(queries, kv_cache, key_scale, fresh_input, kv_weight, lengths, page_list, owners):
    attended = lax.map(lambda group_item: attend_group(group_item, key_scale, kv_weight), (queries, kv_cache, fresh_input, lengths[:, 0].astype(jnp.int32)))
    handed = hand_pages(kv_cache, page_list, owners)
    return (attended, handed)
```

```python
import functools
import math

import jax
import jax.numpy as jnp
from jax import lax
from jax.experimental import pallas as pl
from jax.experimental.pallas import tpu as pltpu
from jax.sharding import PartitionSpec as P

HEADS = 64
KVH = 8
HD = 128
ROWS = 128
CTX = 1024
PAGE = 16
GQ = 8
KVW = 1024
PAGES = CTX // PAGE
FIN = 16
CAP = 2
NX = 4
QUARTERS = 4
QCOLS = 2 * KVW // QUARTERS
CHUNK = 4
CHUNKS = 2 * QUARTERS * FIN // CHUNK
WINDOW = 4

ROPE_BASE = 500000.0
NEG_FILL = -1e30
TO_LOG2 = math.log2(math.e) / math.sqrt(HD)

F32 = jnp.float32
BF16 = jnp.bfloat16
MESH = pl.DeviceIdType.MESH


def rope_tables(positions):
    half_width = HD // 2
    steps_index = jnp.arange(half_width, dtype=jnp.float32)
    inverse = jnp.exp(steps_index * (-2.0 * math.log(ROPE_BASE) / HD))
    angles = positions.astype(jnp.float32)[:, None] * inverse[None, :]
    cosine, sine = jnp.cos(angles), jnp.sin(angles)
    return jnp.concatenate([cosine, cosine], axis=1), jnp.concatenate([-sine, sine], axis=1)


def rotate(values, cosine, sine):
    swapped = jnp.concatenate([values[:, HD // 2 :], values[:, : HD // 2]], axis=1)
    return values * cosine + swapped * sine


def dot_nt(a, b):
    return lax.dot_general(a, b, (((1,), (1,)), ((), ())), preferred_element_type=F32)


def soft_block(scores):
    peak = jnp.max(scores, axis=0, keepdims=True)
    weights = jnp.exp2((scores - peak) * TO_LOG2)
    total = jnp.sum(weights, axis=0, keepdims=True)
    return peak * TO_LOG2, total, weights.astype(BF16)


def merge(parts):
    top = functools.reduce(jnp.maximum, [p[0] for p in parts])
    factors = [jnp.exp2(p[0] - top) for p in parts]
    total = sum(p[1] * f for p, f in zip(parts, factors))
    numerator = sum(p[2] * f for p, f in zip(parts, factors))
    return top, total, numerator


def kernel(
    q_hbm, cache_hbm, fin_hbm, w_hbm, scale_ref, ccos_ref, csin_ref, qcos_ref, qsin_ref, len_ref, plist_ref, own_ref,
    att_ref, handed_ref,
    q_ref, cache_ref, fin_ref, w_ref,
    keys, rows, vals_t,
    xs, xst, xr, xrt, zs, zst, zr, zrt,
    fs, fr, gs, gr,
    page_out, stream, work, picked, meta_out, meta_in, meta,
    load_sem, meta_send, meta_recv, meta_load, page_send, stream_send, stream_recv,
    xs_send, xs_recv, xt_send, xt_recv, zs_send, zs_recv, zt_send, zt_recv,
    f_send, f_recv, g_send, g_recv, pick_send, pick_recv, own_sem,
):
    sec, grp, rank = lax.axis_index("sec"), lax.axis_index("grp"), lax.axis_index("rank")
    x, z = lax.div(rank, NX), lax.rem(rank, NX)

    def at(xx, zz, section=None):
        return (sec if section is None else section, grp, xx * NX + zz)

    def remote(src, dst, send, recv, device):
        return pltpu.make_async_remote_copy(
            src_ref=src, dst_ref=dst, send_sem=send, recv_sem=recv, device_id=device, device_id_type=MESH
        )

    def plus(value, by):
        return lax.rem(value + by, NX)

    loads = [
        pltpu.make_async_copy(src, dst, load_sem.at[i])
        for i, (src, dst) in enumerate(
            ((cache_hbm, cache_ref), (fin_hbm, fin_ref), (w_hbm, w_ref), (q_hbm, q_ref))
        )
    ]
    for load in loads:
        load.start()

    barrier = pltpu.get_barrier_semaphore()
    for o in range(1, NX):
        pl.semaphore_signal(barrier, inc=1, device_id=at(plus(x, o), z), device_id_type=MESH)
        pl.semaphore_signal(barrier, inc=1, device_id=at(x, plus(z, o)), device_id_type=MESH)
    for zz in range(NX):
        pl.semaphore_signal(barrier, inc=1, device_id=at(x, zz, 1 - sec), device_id_type=MESH)

    rightward = z >= NX // 2
    entry = jnp.where(rightward, 0, NX - 1)
    lane = jnp.where(rightward, 0, 1)
    nearness = jnp.where(rightward, NX - 1 - z, z)

    def page_copy(m):
        n = lax.div(m, FIN // CHUNK) * (2 * FIN // CHUNK) + lax.rem(m, FIN // CHUNK) * 2 + nearness
        return remote(
            page_out.at[m], stream.at[lane, n], page_send.at[m], stream_recv.at[lane, n], at(x, entry, 1)
        )

    def meta_copy(zz):
        return remote(meta_out, meta_in.at[z], meta_send.at[zz], meta_recv.at[z], at(x, zz, 1))

    loads[0].wait()

    @pl.when(sec == 0)
    def _():
        lanes = lax.broadcasted_iota(jnp.int32, (8, 128), 1)
        owner_of, slot_of = lanes // CAP, lanes % CAP
        count = jnp.zeros((8, 128), jnp.int32)
        chosen = jnp.full((8, 128), FIN, jnp.int32)
        for f in range(FIN):
            mine = owner_of == own_ref[f]
            chosen = jnp.where(mine & (count == slot_of), f, chosen)
            count = count + jnp.where(mine, 1, 0)
        meta_out[...] = chosen

        @pl.loop(0, FIN)
        def _(f):
            page = plist_ref[f]
            for part in range(QUARTERS):
                page_out[part * (FIN // CHUNK) + lax.div(f, CHUNK), lax.rem(f, CHUNK)] = cache_ref[
                    page, :, part * QCOLS : (part + 1) * QCOLS
                ]

    pl.semaphore_wait(barrier, 2 * (NX - 1) + NX)

    @pl.when(sec == 0)
    def _():
        for zz in range(NX):
            meta_copy(zz).start()
        for m in range(WINDOW):
            page_copy(m).start()

    loads[1].wait()
    loads[2].wait()

    def fresh_x(xx):
        o = plus(xx - x + NX, 0)
        return remote(fs.at[xx], fr.at[o], f_send.at[o], f_recv.at[o], at(xx, z))

    for xx in range(NX):
        for kind in range(2):
            cols = slice(kind * KVW + xx * 2 * HD, kind * KVW + (xx + 1) * 2 * HD)
            fs[xx, kind] = jnp.dot(fin_ref[...], w_ref[:, cols], preferred_element_type=F32)

        @pl.when(xx != x)
        def _():
            fresh_x(xx).start()

    def fresh_z(zz):
        o = plus(zz - z + NX, 0)
        return remote(gs.at[zz // 2], gr.at[o], g_send.at[o], g_recv.at[o], at(x, zz))

    def fresh_sum_x():
        for o in range(1, NX):
            remote(fs.at[0], fr.at[o], f_send.at[o], f_recv.at[o], at(plus(x, o), z)).wait_recv()
        for kind in range(2):
            total = fs[x, kind] + fr[1, kind] + fr[2, kind] + fr[3, kind]
            gs[0, kind] = total[:, :HD]
            gs[1, kind] = total[:, HD:]
        for zz in range(NX):

            @pl.when(zz != z)
            def _():
                fresh_z(zz).start()

    def stream_copy(d, n):
        onward = jnp.minimum(z + 1, NX - 1) if d == 0 else jnp.maximum(z - 1, 0)
        return remote(
            stream.at[d, n], stream.at[d, n], stream_send.at[d, n], stream_recv.at[d, n], at(x, onward, 1)
        )

    def stream_step(n):
        for d in range(2):
            stream_copy(d, n).wait_recv()

            @pl.when((z < NX - 1) if d == 0 else (z > 0))
            def _():
                stream_copy(d, n).start()

    def picked_copy(part, o):
        xx = plus(x, o)
        return remote(
            picked.at[part, pl.ds(xx * 8, 8)],
            handed_ref.at[pl.ds(x * 8, 8), :, pl.ds(part * QCOLS, QCOLS)],
            pick_send.at[part, o],
            pick_recv.at[part, o],
            at(xx, z, 1),
        )

    def picked_own(part):
        return pltpu.make_async_copy(
            picked.at[part, pl.ds(x * 8, 8)],
            handed_ref.at[pl.ds(x * 8, 8), :, pl.ds(part * QCOLS, QCOLS)],
            own_sem.at[part],
        )

    def dispatch(part):
        for zz in range(NX):
            d, s = (0, NX - 1 - zz) if zz >= NX // 2 else (1, zz)

            @pl.loop(0, FIN)
            def _(f):
                n = part * (2 * FIN // CHUNK) + lax.div(f, CHUNK) * 2 + s
                work[zz, f] = stream[d, n, lax.rem(f, CHUNK)]

        @pl.loop(0, NX)
        def _(xx):
            for zz in range(NX):
                for c in range(CAP):
                    index = meta[zz, 0, (xx * NX + z) * CAP + c]
                    picked[part, xx * 8 + zz * CAP + c] = work[zz, index]

        for o in range(1, NX):
            picked_copy(part, o).start()
        picked_own(part).start()

    @pl.when(sec == 1)
    def _():
        for zz in range(NX):
            work[zz, FIN] = jnp.zeros((PAGE, QCOLS), BF16)

    loads[3].wait()
    edge = len_ref[0] - rank * CTX
    inside = lax.broadcasted_iota(jnp.int32, (CTX, HD), 0) < edge
    first = lax.broadcasted_iota(jnp.int32, (CTX, HD), 1) == 0
    keys[:, HD:] = jnp.where(first & jnp.logical_not(inside), NEG_FILL, 0.0).astype(BF16)
    rows[:, HD:] = jnp.where(first, 1.0, 0.0).astype(BF16)

    def xs_copy(o):
        xx = plus(x, o)
        return (
            remote(xs.at[xx], xr.at[o], xs_send.at[o], xs_recv.at[o], at(xx, z)),
            remote(xst.at[xx], xrt.at[o], xt_send.at[o], xt_recv.at[o], at(xx, z)),
        )

    @pl.loop(0, 2 * KVH)
    def _(u):
        j, half = lax.div(u, 2), lax.rem(u, 2)
        o = plus(lax.div(j, 2), 1)
        xx, hh = plus(x, o), lax.rem(j, 2)
        head = xx * 2 + hh

        @pl.when(half == 0)
        def _():
            cols = pl.ds(pl.multiple_of(head * HD, HD), HD)
            raw = cache_ref[:, :, cols].reshape(CTX, HD).astype(F32) * scale_ref[:, cols]
            keys[:, :HD] = rotate(raw, ccos_ref[...], csin_ref[...]).astype(BF16)
            val_cols = pl.ds(pl.multiple_of(KVW + head * HD, HD), HD)
            vals_t[...] = cache_ref[:, :, val_cols].reshape(CTX, HD).T
            for g in range(GQ):
                q_cols = pl.ds(pl.multiple_of((head * GQ + g) * HD, HD), HD)
                rows[g * ROWS : (g + 1) * ROWS, :HD] = rotate(
                    q_ref[:, q_cols].astype(F32), qcos_ref[...], qsin_ref[...]
                ).astype(BF16)

        for b in range(2):
            cols = pl.ds(pl.multiple_of(half * 512 + b * 256, 256), 256)
            scores = dot_nt(keys[...], rows[cols, :])
            peak, total, weights = soft_block(scores)
            numerator = jnp.dot(vals_t[...], weights, preferred_element_type=F32)
            xs[xx, hh, :, cols] = numerator.astype(BF16)
            for h in range(2):

                @pl.when(hh == h)
                def _():
                    xst[xx, 2 * h : 2 * h + 1, cols] = peak
                    xst[xx, 2 * h + 1 : 2 * h + 2, cols] = total

        @pl.when((lax.rem(u, 4) == 3) & (o != 0))
        def _():
            for copy in xs_copy(o):
                copy.start()

        @pl.when(sec == 0)
        def _():
            page_copy(u).wait_send()

            @pl.when(u + WINDOW < FIN)
            def _():
                page_copy(u + WINDOW).start()

        @pl.when(sec == 1)
        def _():
            stream_step(u)

        @pl.when(u == 8)
        def _():
            fresh_sum_x()

        @pl.when((sec == 1) & (u == 9))
        def _():
            for zz in range(NX):
                remote(meta_out, meta_in.at[zz], meta_send.at[zz], meta_recv.at[zz], at(x, zz, 0)).wait_recv()
            load = pltpu.make_async_copy(meta_in, meta, meta_load)
            load.start()
            load.wait()
            dispatch(0)

    @pl.when(sec == 0)
    def _():
        picked[0] = jnp.zeros((2 * FIN, PAGE, QCOLS), BF16)
        for part in range(QUARTERS):
            pltpu.make_async_copy(
                picked.at[0], handed_ref.at[:, :, pl.ds(part * QCOLS, QCOLS)], own_sem.at[part]
            ).start()

    @pl.when(sec == 1)
    def _():
        dispatch(1)

    for o in range(1, NX):
        for copy in xs_copy(o):
            copy.wait_recv()

    def zs_copy(zz):
        o = plus(zz - z + NX, 0)
        return (
            remote(zs.at[zz], zr.at[o], zs_send.at[o], zs_recv.at[o], at(x, zz)),
            remote(zst.at[zz], zrt.at[o], zt_send.at[o], zt_recv.at[o], at(x, zz)),
        )

    for zz in range(NX):
        hh, cols = zz // 2, slice((zz % 2) * 512, (zz % 2 + 1) * 512)
        parts = [
            (xst[x, 2 * hh : 2 * hh + 1, cols], xst[x, 2 * hh + 1 : 2 * hh + 2, cols], xs[x, hh, :, cols].astype(F32))
        ]
        for o in range(1, NX):
            parts.append(
                (
                    xrt[o, 2 * hh : 2 * hh + 1, cols],
                    xrt[o, 2 * hh + 1 : 2 * hh + 2, cols],
                    xr[o, hh, :, cols].astype(F32),
                )
            )
        top, total, numerator = merge(parts)
        zs[zz] = numerator.astype(BF16)
        zst[zz, 0:1, :] = top
        zst[zz, 1:2, :] = total

        @pl.when(zz != z)
        def _():
            for copy in zs_copy(zz):
                copy.start()

    for o in range(1, NX):
        remote(gs.at[0], gr.at[o], g_send.at[o], g_recv.at[o], at(x, plus(z, o))).wait_recv()
    mine = lax.div(z, 2)
    fresh = [(gs[mine, kind] + gr[1, kind] + gr[2, kind] + gr[3, kind]).astype(BF16) for kind in range(2)]
    fresh_keys = rotate(fresh[0].astype(F32), qcos_ref[...], qsin_ref[...]).astype(BF16)
    own_rows = []
    for h in range(HEADS // (NX * NX)):
        q_cols = pl.ds(pl.multiple_of((rank * 4 + h) * HD, HD), HD)
        own_rows.append(rotate(q_ref[:, q_cols].astype(F32), qcos_ref[...], qsin_ref[...]).astype(BF16))
    scores = dot_nt(fresh_keys, jnp.concatenate(own_rows, axis=0))
    key_row = lax.broadcasted_iota(jnp.int32, scores.shape, 0)
    query_row = lax.broadcasted_iota(jnp.int32, scores.shape, 1) % ROWS
    peak, total, weights = soft_block(jnp.where(key_row <= query_row, scores, NEG_FILL))
    numerator = jnp.dot(fresh[1].astype(F32).T.astype(BF16), weights, preferred_element_type=F32)
    parts = [(peak, total, numerator)]

    @pl.when(sec == 1)
    def _():
        @pl.loop(16, 24)
        def _(n):
            stream_step(n)

        dispatch(2)

    for o in range(1, NX):
        for copy in zs_copy(plus(z, o)):
            copy.wait_recv()
    parts.append((zst[z, 0:1, :], zst[z, 1:2, :], zs[z].astype(F32)))
    for o in range(1, NX):
        parts.append((zrt[o, 0:1, :], zrt[o, 1:2, :], zr[o].astype(F32)))
    _, total, numerator = merge(parts)
    result = numerator / total
    for h in range(HEADS // (NX * NX)):
        att_ref[0, :, h * HD : (h + 1) * HD] = result[:, h * ROWS : (h + 1) * ROWS].T.astype(BF16)

    @pl.when(sec == 1)
    def _():
        @pl.loop(24, 32)
        def _(n):
            stream_step(n)

        dispatch(3)

    for o in range(1, NX):
        for copy in xs_copy(o):
            copy.wait_send()
        for copy in zs_copy(plus(z, o)):
            copy.wait_send()
        fresh_x(plus(x, o)).wait_send()
        remote(gs.at[0], gr.at[o], g_send.at[o], g_recv.at[o], at(x, plus(z, o))).wait_send()

    @pl.when(sec == 0)
    def _():
        for zz in range(NX):
            meta_copy(zz).wait_send()
        for part in range(QUARTERS):
            pltpu.make_async_copy(
                picked.at[0], handed_ref.at[:, :, pl.ds(part * QCOLS, QCOLS)], own_sem.at[part]
            ).wait()

    @pl.when(sec == 1)
    def _():
        for d in range(2):

            @pl.when((z < NX - 1) if d == 0 else (z > 0))
            def _():
                @pl.loop(0, CHUNKS)
                def _(n):
                    stream_copy(d, n).wait_send()

        for part in range(QUARTERS):
            for o in range(1, NX):
                picked_copy(part, o).wait_send()
                picked_copy(part, o).wait_recv()
            picked_own(part).wait()


def shards(queries, kv_cache, key_scale, fresh_input, kv_weight, lengths, page_list, owners):
    position = lax.axis_index("rank")
    length = lengths[0, 0]
    qcos, qsin = rope_tables(length + jnp.arange(ROWS, dtype=jnp.int32))
    ccos, csin = rope_tables(position * CTX + jnp.arange(CTX, dtype=jnp.int32))
    whole = pl.BlockSpec(memory_space=pltpu.VMEM)
    scalars = pl.BlockSpec(memory_space=pltpu.SMEM)
    anywhere = pl.BlockSpec(memory_space=pl.ANY)
    dma = pltpu.SemaphoreType.DMA
    attended, handed = pl.pallas_call(
        kernel,
        out_shape=(
            jax.ShapeDtypeStruct((1, ROWS, 512), BF16),
            jax.ShapeDtypeStruct((2 * FIN, PAGE, 2 * KVW), BF16),
        ),
        in_specs=[anywhere] * 4 + [whole] * 5 + [scalars] * 3,
        out_specs=(whole, anywhere),
        scratch_shapes=[
            pltpu.VMEM((ROWS, HEADS * HD), BF16),
            pltpu.VMEM((PAGES, PAGE, 2 * KVW), BF16),
            pltpu.VMEM((ROWS, 512), BF16),
            pltpu.VMEM((512, 2 * KVW), BF16),
            pltpu.VMEM((CTX, 2 * HD), BF16),
            pltpu.VMEM((CTX, 2 * HD), BF16),
            pltpu.VMEM((HD, CTX), BF16),
            pltpu.VMEM((NX, 2, HD, CTX), BF16),
            pltpu.VMEM((NX, 8, CTX), F32),
            pltpu.VMEM((NX, 2, HD, CTX), BF16),
            pltpu.VMEM((NX, 8, CTX), F32),
            pltpu.VMEM((NX, HD, 512), BF16),
            pltpu.VMEM((NX, 8, 512), F32),
            pltpu.VMEM((NX, HD, 512), BF16),
            pltpu.VMEM((NX, 8, 512), F32),
            pltpu.VMEM((NX, 2, ROWS, 2 * HD), F32),
            pltpu.VMEM((NX, 2, ROWS, 2 * HD), F32),
            pltpu.VMEM((2, 2, ROWS, HD), F32),
            pltpu.VMEM((NX, 2, ROWS, HD), F32),
            pltpu.VMEM((CHUNKS // 2, CHUNK, PAGE, QCOLS), BF16),
            pltpu.VMEM((2, CHUNKS, CHUNK, PAGE, QCOLS), BF16),
            pltpu.VMEM((NX, FIN + 1, PAGE, QCOLS), BF16),
            pltpu.VMEM((QUARTERS, 2 * FIN, PAGE, QCOLS), BF16),
            pltpu.VMEM((8, 128), jnp.int32),
            pltpu.VMEM((NX, 8, 128), jnp.int32),
            pltpu.SMEM((NX, 8, 128), jnp.int32),
            dma((4,)),
            dma((NX,)),
            dma((NX,)),
            dma,
            dma((CHUNKS // 2,)),
            dma((2, CHUNKS)),
            dma((2, CHUNKS)),
        ]
        + [dma((NX,))] * 12
        + [dma((QUARTERS, NX)), dma((QUARTERS, NX)), dma((QUARTERS,))],
        compiler_params=pltpu.CompilerParams(
            collective_id=0, has_side_effects=True, vmem_limit_bytes=56 * 1024 * 1024
        ),
        cost_estimate=pl.CostEstimate(flops=4_500_000_000, bytes_accessed=12_000_000, transcendentals=8_500_000),
        name="attend_and_hand",
    )(
        queries[0],
        kv_cache.reshape(PAGES, PAGE, 2 * KVW),
        fresh_input[0],
        kv_weight,
        key_scale.reshape(1, KVW),
        ccos,
        csin,
        qcos,
        qsin,
        lengths.reshape(1),
        page_list,
        owners.reshape(FIN),
    )
    return attended, handed[None]


def solution(mesh):
    return jax.shard_map(
        shards,
        mesh=mesh,
        in_specs=(
            P(("sec", "grp"), None, None),
            P(("sec", "grp"), "rank", None),
            P(),
            P(("sec", "grp"), None, "rank"),
            P("rank", None),
            P(("sec", "grp"), None),
            P(("sec", "grp", "rank")),
            P(("sec", "grp", "rank"), None),
        ),
        out_specs=(P(("sec", "grp"), None, "rank"), P(("sec", "grp", "rank"), None, None, None)),
        check_vma=False,
    )
```

```python
import functools
import math

import jax
import jax.numpy as jnp
from jax import lax
from jax.experimental import pallas as pl
from jax.experimental.pallas import tpu as pltpu
from jax.sharding import PartitionSpec as P

HEADS = 64
KVH = 8
HD = 128
ROWS = 128
CTX = 1024
PAGE = 16
GQ = 8
KVW = 1024
PAGES = CTX // PAGE
FIN = 16
CAP = 2
NX = 4
QUARTERS = 4
QCOLS = 2 * KVW // QUARTERS
CHUNK = 4
CHUNKS = 2 * QUARTERS * FIN // CHUNK
WINDOW = 4
SKEW = 2
PER_UNIT = 1
UNITS = 2 * KVH

ROPE_BASE = 500000.0
NEG_FILL = -1e30
TO_LOG2 = math.log2(math.e) / math.sqrt(HD)

F32 = jnp.float32
BF16 = jnp.bfloat16
MESH = pl.DeviceIdType.MESH


def rope_tables(positions):
    half_width = HD // 2
    steps_index = jnp.arange(half_width, dtype=jnp.float32)
    inverse = jnp.exp(steps_index * (-2.0 * math.log(ROPE_BASE) / HD))
    angles = positions.astype(jnp.float32)[:, None] * inverse[None, :]
    cosine, sine = jnp.cos(angles), jnp.sin(angles)
    return jnp.concatenate([cosine, cosine], axis=1), jnp.concatenate([-sine, sine], axis=1)


def rotate(values, cosine, sine):
    swapped = jnp.concatenate([values[:, HD // 2 :], values[:, : HD // 2]], axis=1)
    return values * cosine + swapped * sine


def dot_nt(a, b):
    return lax.dot_general(a, b, (((1,), (1,)), ((), ())), preferred_element_type=F32)


def soft_block(scores):
    peak = jnp.max(scores, axis=0, keepdims=True)
    weights = jnp.exp2((scores - peak) * TO_LOG2)
    total = jnp.sum(weights, axis=0, keepdims=True)
    return peak * TO_LOG2, total, weights.astype(BF16)


def merge(parts):
    top = functools.reduce(jnp.maximum, [p[0] for p in parts])
    factors = [jnp.exp2(p[0] - top) for p in parts]
    total = sum(p[1] * f for p, f in zip(parts, factors))
    numerator = sum(p[2] * f for p, f in zip(parts, factors))
    return top, total, numerator


def steps_for(part):
    return (part + 1) * CHUNKS // QUARTERS + SKEW * (NX - 1)


def kernel(
    q_hbm, cache_hbm, fin_hbm, w_hbm, scale_ref, ccos_ref, csin_ref, qcos_ref, qsin_ref, len_ref, plist_ref, own_ref,
    att_ref, handed_ref,
    q_ref, cache_ref, fin_ref, w_ref,
    keys, rows, vals_t,
    xs, xst, xr, xrt, zs, zst, zr, zrt,
    fs, fr, gs, gr,
    page_out, stream, work, picked, meta_out, meta_in, meta,
    load_sem, meta_send, meta_recv, meta_load, page_send, stream_send, stream_recv,
    xs_send, xs_recv, xt_send, xt_recv, zs_send, zs_recv, zt_send, zt_recv,
    f_send, f_recv, g_send, g_recv, pick_send, pick_recv, own_sem,
):
    sec, grp, rank = lax.axis_index("sec"), lax.axis_index("grp"), lax.axis_index("rank")
    x, z = lax.div(rank, NX), lax.rem(rank, NX)

    def at(xx, zz, section=None):
        return (sec if section is None else section, grp, xx * NX + zz)

    def remote(src, dst, send, recv, device):
        return pltpu.make_async_remote_copy(
            src_ref=src, dst_ref=dst, send_sem=send, recv_sem=recv, device_id=device, device_id_type=MESH
        )

    def plus(value, by):
        return lax.rem(value + by, NX)

    loads = [
        pltpu.make_async_copy(src, dst, load_sem.at[i])
        for i, (src, dst) in enumerate(
            ((cache_hbm, cache_ref), (fin_hbm, fin_ref), (w_hbm, w_ref), (q_hbm, q_ref))
        )
    ]
    for load in loads:
        load.start()

    barrier = pltpu.get_barrier_semaphore()
    for o in range(1, NX):
        pl.semaphore_signal(barrier, inc=1, device_id=at(plus(x, o), z), device_id_type=MESH)
        pl.semaphore_signal(barrier, inc=1, device_id=at(x, plus(z, o)), device_id_type=MESH)
    for zz in range(NX):
        pl.semaphore_signal(barrier, inc=1, device_id=at(x, zz, 1 - sec), device_id_type=MESH)

    rightward = z >= NX // 2
    entry = jnp.where(rightward, 0, NX - 1)
    lane = jnp.where(rightward, 0, 1)
    nearness = jnp.where(rightward, NX - 1 - z, z)

    def page_copy(m):
        n = lax.div(m, FIN // CHUNK) * (2 * FIN // CHUNK) + lax.rem(m, FIN // CHUNK) * 2 + nearness
        return remote(
            page_out.at[m], stream.at[lane, n], page_send.at[m], stream_recv.at[lane, n], at(x, entry, 1)
        )

    def meta_copy(zz):
        return remote(meta_out, meta_in.at[z], meta_send.at[zz], meta_recv.at[z], at(x, zz, 1))

    loads[0].wait()

    @pl.when(sec == 0)
    def _():
        lanes = lax.broadcasted_iota(jnp.int32, (8, 128), 1)
        owner_of, slot_of = lanes // CAP, lanes % CAP
        count = jnp.zeros((8, 128), jnp.int32)
        chosen = jnp.full((8, 128), FIN, jnp.int32)
        for f in range(FIN):
            mine = owner_of == own_ref[f]
            chosen = jnp.where(mine & (count == slot_of), f, chosen)
            count = count + jnp.where(mine, 1, 0)
        meta_out[...] = chosen

        @pl.loop(0, FIN)
        def _(f):
            page = plist_ref[f]
            for part in range(QUARTERS):
                page_out[part * (FIN // CHUNK) + lax.div(f, CHUNK), lax.rem(f, CHUNK)] = cache_ref[
                    page, :, part * QCOLS : (part + 1) * QCOLS
                ]

    pl.semaphore_wait(barrier, 2 * (NX - 1) + NX)

    @pl.when(sec == 0)
    def _():
        for zz in range(NX):
            meta_copy(zz).start()
        for m in range(WINDOW):
            page_copy(m).start()

    loads[1].wait()
    loads[2].wait()

    def fresh_x(xx):
        o = plus(xx - x + NX, 0)
        return remote(fs.at[xx], fr.at[o], f_send.at[o], f_recv.at[o], at(xx, z))

    for xx in range(NX):
        for kind in range(2):
            cols = slice(kind * KVW + xx * 2 * HD, kind * KVW + (xx + 1) * 2 * HD)
            fs[xx, kind] = jnp.dot(fin_ref[...], w_ref[:, cols], preferred_element_type=F32)

        @pl.when(xx != x)
        def _():
            fresh_x(xx).start()

    def fresh_z(zz):
        o = plus(zz - z + NX, 0)
        return remote(gs.at[zz // 2], gr.at[o], g_send.at[o], g_recv.at[o], at(x, zz))

    def fresh_sum_x():
        for o in range(1, NX):
            remote(fs.at[0], fr.at[o], f_send.at[o], f_recv.at[o], at(plus(x, o), z)).wait_recv()
        for kind in range(2):
            total = fs[x, kind] + fr[1, kind] + fr[2, kind] + fr[3, kind]
            gs[0, kind] = total[:, :HD]
            gs[1, kind] = total[:, HD:]
        for zz in range(NX):

            @pl.when(zz != z)
            def _():
                fresh_z(zz).start()

    def stream_copy(d, n):
        onward = jnp.minimum(z + 1, NX - 1) if d == 0 else jnp.maximum(z - 1, 0)
        return remote(
            stream.at[d, n], stream.at[d, n], stream_send.at[d, n], stream_recv.at[d, n], at(x, onward, 1)
        )

    def stream_step(step):
        for d in range(2):
            n = step - SKEW * (z if d == 0 else NX - 1 - z)

            @pl.when((n >= 0) & (n < CHUNKS))
            def _():
                stream_copy(d, n).wait_recv()

                @pl.when((z < NX - 1) if d == 0 else (z > 0))
                def _():
                    stream_copy(d, n).start()

    def stream_until(part, begun):
        @pl.loop(begun, steps_for(part))
        def _(step):
            stream_step(step)

        dispatch(part)

    def picked_copy(part, o):
        xx = plus(x, o)
        return remote(
            picked.at[part, pl.ds(xx * 8, 8)],
            handed_ref.at[pl.ds(x * 8, 8), :, pl.ds(part * QCOLS, QCOLS)],
            pick_send.at[part, o],
            pick_recv.at[part, o],
            at(xx, z, 1),
        )

    def picked_own(part):
        return pltpu.make_async_copy(
            picked.at[part, pl.ds(x * 8, 8)],
            handed_ref.at[pl.ds(x * 8, 8), :, pl.ds(part * QCOLS, QCOLS)],
            own_sem.at[part],
        )

    def dispatch(part):
        for zz in range(NX):
            d, s = (0, NX - 1 - zz) if zz >= NX // 2 else (1, zz)

            @pl.loop(0, FIN)
            def _(f):
                n = part * (2 * FIN // CHUNK) + lax.div(f, CHUNK) * 2 + s
                work[zz, f] = stream[d, n, lax.rem(f, CHUNK)]

        @pl.loop(0, NX)
        def _(xx):
            for zz in range(NX):
                for c in range(CAP):
                    index = meta[zz, 0, (xx * NX + z) * CAP + c]
                    picked[part, xx * 8 + zz * CAP + c] = work[zz, index]

        for o in range(1, NX):
            picked_copy(part, o).start()
        picked_own(part).start()

    @pl.when(sec == 1)
    def _():
        for zz in range(NX):
            work[zz, FIN] = jnp.zeros((PAGE, QCOLS), BF16)

    loads[3].wait()
    edge = len_ref[0] - rank * CTX
    inside = lax.broadcasted_iota(jnp.int32, (CTX, HD), 0) < edge
    first = lax.broadcasted_iota(jnp.int32, (CTX, HD), 1) == 0
    keys[:, HD:] = jnp.where(first & jnp.logical_not(inside), NEG_FILL, 0.0).astype(BF16)
    rows[:, HD:] = jnp.where(first, 1.0, 0.0).astype(BF16)

    def xs_copy(o):
        xx = plus(x, o)
        return (
            remote(xs.at[xx], xr.at[o], xs_send.at[o], xs_recv.at[o], at(xx, z)),
            remote(xst.at[xx], xrt.at[o], xt_send.at[o], xt_recv.at[o], at(xx, z)),
        )

    @pl.loop(0, UNITS)
    def _(u):
        j, half = lax.div(u, 2), lax.rem(u, 2)
        o = plus(lax.div(j, 2), 1)
        xx, hh = plus(x, o), lax.rem(j, 2)
        head = xx * 2 + hh

        @pl.when(half == 0)
        def _():
            cols = pl.ds(pl.multiple_of(head * HD, HD), HD)
            raw = cache_ref[:, :, cols].reshape(CTX, HD).astype(F32) * scale_ref[:, cols]
            keys[:, :HD] = rotate(raw, ccos_ref[...], csin_ref[...]).astype(BF16)
            val_cols = pl.ds(pl.multiple_of(KVW + head * HD, HD), HD)
            vals_t[...] = cache_ref[:, :, val_cols].reshape(CTX, HD).T
            for g in range(GQ):
                q_cols = pl.ds(pl.multiple_of((head * GQ + g) * HD, HD), HD)
                rows[g * ROWS : (g + 1) * ROWS, :HD] = rotate(
                    q_ref[:, q_cols].astype(F32), qcos_ref[...], qsin_ref[...]
                ).astype(BF16)

        for b in range(2):
            cols = pl.ds(pl.multiple_of(half * 512 + b * 256, 256), 256)
            scores = dot_nt(keys[...], rows[cols, :])
            peak, total, weights = soft_block(scores)
            numerator = jnp.dot(vals_t[...], weights, preferred_element_type=F32)
            xs[xx, hh, :, cols] = numerator.astype(BF16)
            for h in range(2):

                @pl.when(hh == h)
                def _():
                    xst[xx, 2 * h : 2 * h + 1, cols] = peak
                    xst[xx, 2 * h + 1 : 2 * h + 2, cols] = total

        @pl.when((lax.rem(u, 4) == 3) & (o != 0))
        def _():
            for copy in xs_copy(o):
                copy.start()

        @pl.when(sec == 0)
        def _():
            page_copy(u).wait_send()

            @pl.when(u + WINDOW < FIN)
            def _():
                page_copy(u + WINDOW).start()

        @pl.when(sec == 1)
        def _():
            for i in range(PER_UNIT):
                stream_step(u * PER_UNIT + i)

        @pl.when(u == 8)
        def _():
            fresh_sum_x()

        @pl.when((sec == 1) & ((u + 1) * PER_UNIT == steps_for(0)))
        def _():
            for zz in range(NX):
                remote(meta_out, meta_in.at[zz], meta_send.at[zz], meta_recv.at[zz], at(x, zz, 0)).wait_recv()
            load = pltpu.make_async_copy(meta_in, meta, meta_load)
            load.start()
            load.wait()
            dispatch(0)

    @pl.when(sec == 0)
    def _():
        picked[0] = jnp.zeros((2 * FIN, PAGE, QCOLS), BF16)
        for part in range(QUARTERS):
            pltpu.make_async_copy(
                picked.at[0], handed_ref.at[:, :, pl.ds(part * QCOLS, QCOLS)], own_sem.at[part]
            ).start()

    @pl.when(sec == 1)
    def _():
        stream_until(1, UNITS * PER_UNIT)

    for o in range(1, NX):
        for copy in xs_copy(o):
            copy.wait_recv()

    def zs_copy(zz):
        o = plus(zz - z + NX, 0)
        return (
            remote(zs.at[zz], zr.at[o], zs_send.at[o], zs_recv.at[o], at(x, zz)),
            remote(zst.at[zz], zrt.at[o], zt_send.at[o], zt_recv.at[o], at(x, zz)),
        )

    for zz in range(NX):
        hh, cols = zz // 2, slice((zz % 2) * 512, (zz % 2 + 1) * 512)
        parts = [
            (xst[x, 2 * hh : 2 * hh + 1, cols], xst[x, 2 * hh + 1 : 2 * hh + 2, cols], xs[x, hh, :, cols].astype(F32))
        ]
        for o in range(1, NX):
            parts.append(
                (
                    xrt[o, 2 * hh : 2 * hh + 1, cols],
                    xrt[o, 2 * hh + 1 : 2 * hh + 2, cols],
                    xr[o, hh, :, cols].astype(F32),
                )
            )
        top, total, numerator = merge(parts)
        zs[zz] = numerator.astype(BF16)
        zst[zz, 0:1, :] = top
        zst[zz, 1:2, :] = total

        @pl.when(zz != z)
        def _():
            for copy in zs_copy(zz):
                copy.start()

    for o in range(1, NX):
        remote(gs.at[0], gr.at[o], g_send.at[o], g_recv.at[o], at(x, plus(z, o))).wait_recv()
    mine = lax.div(z, 2)
    fresh = [(gs[mine, kind] + gr[1, kind] + gr[2, kind] + gr[3, kind]).astype(BF16) for kind in range(2)]
    fresh_keys = rotate(fresh[0].astype(F32), qcos_ref[...], qsin_ref[...]).astype(BF16)
    own_rows = []
    for h in range(HEADS // (NX * NX)):
        q_cols = pl.ds(pl.multiple_of((rank * 4 + h) * HD, HD), HD)
        own_rows.append(rotate(q_ref[:, q_cols].astype(F32), qcos_ref[...], qsin_ref[...]).astype(BF16))
    scores = dot_nt(fresh_keys, jnp.concatenate(own_rows, axis=0))
    key_row = lax.broadcasted_iota(jnp.int32, scores.shape, 0)
    query_row = lax.broadcasted_iota(jnp.int32, scores.shape, 1) % ROWS
    peak, total, weights = soft_block(jnp.where(key_row <= query_row, scores, NEG_FILL))
    numerator = jnp.dot(fresh[1].astype(F32).T.astype(BF16), weights, preferred_element_type=F32)
    parts = [(peak, total, numerator)]

    @pl.when(sec == 1)
    def _():
        stream_until(2, steps_for(1))

    for o in range(1, NX):
        for copy in zs_copy(plus(z, o)):
            copy.wait_recv()
    parts.append((zst[z, 0:1, :], zst[z, 1:2, :], zs[z].astype(F32)))
    for o in range(1, NX):
        parts.append((zrt[o, 0:1, :], zrt[o, 1:2, :], zr[o].astype(F32)))
    _, total, numerator = merge(parts)
    result = numerator / total
    for h in range(HEADS // (NX * NX)):
        att_ref[0, :, h * HD : (h + 1) * HD] = result[:, h * ROWS : (h + 1) * ROWS].T.astype(BF16)

    @pl.when(sec == 1)
    def _():
        stream_until(3, steps_for(2))

    for o in range(1, NX):
        for copy in xs_copy(o):
            copy.wait_send()
        for copy in zs_copy(plus(z, o)):
            copy.wait_send()
        fresh_x(plus(x, o)).wait_send()
        remote(gs.at[0], gr.at[o], g_send.at[o], g_recv.at[o], at(x, plus(z, o))).wait_send()

    @pl.when(sec == 0)
    def _():
        for zz in range(NX):
            meta_copy(zz).wait_send()
        for part in range(QUARTERS):
            pltpu.make_async_copy(
                picked.at[0], handed_ref.at[:, :, pl.ds(part * QCOLS, QCOLS)], own_sem.at[part]
            ).wait()

    @pl.when(sec == 1)
    def _():
        for d in range(2):

            @pl.when((z < NX - 1) if d == 0 else (z > 0))
            def _():
                @pl.loop(0, CHUNKS)
                def _(n):
                    stream_copy(d, n).wait_send()

        for part in range(QUARTERS):
            for o in range(1, NX):
                picked_copy(part, o).wait_send()
                picked_copy(part, o).wait_recv()
            picked_own(part).wait()


def shards(queries, kv_cache, key_scale, fresh_input, kv_weight, lengths, page_list, owners):
    position = lax.axis_index("rank")
    length = lengths[0, 0]
    qcos, qsin = rope_tables(length + jnp.arange(ROWS, dtype=jnp.int32))
    ccos, csin = rope_tables(position * CTX + jnp.arange(CTX, dtype=jnp.int32))
    whole = pl.BlockSpec(memory_space=pltpu.VMEM)
    scalars = pl.BlockSpec(memory_space=pltpu.SMEM)
    anywhere = pl.BlockSpec(memory_space=pl.ANY)
    dma = pltpu.SemaphoreType.DMA
    attended, handed = pl.pallas_call(
        kernel,
        out_shape=(
            jax.ShapeDtypeStruct((1, ROWS, 512), BF16),
            jax.ShapeDtypeStruct((2 * FIN, PAGE, 2 * KVW), BF16),
        ),
        in_specs=[anywhere] * 4 + [whole] * 5 + [scalars] * 3,
        out_specs=(whole, anywhere),
        scratch_shapes=[
            pltpu.VMEM((ROWS, HEADS * HD), BF16),
            pltpu.VMEM((PAGES, PAGE, 2 * KVW), BF16),
            pltpu.VMEM((ROWS, 512), BF16),
            pltpu.VMEM((512, 2 * KVW), BF16),
            pltpu.VMEM((CTX, 2 * HD), BF16),
            pltpu.VMEM((CTX, 2 * HD), BF16),
            pltpu.VMEM((HD, CTX), BF16),
            pltpu.VMEM((NX, 2, HD, CTX), BF16),
            pltpu.VMEM((NX, 8, CTX), F32),
            pltpu.VMEM((NX, 2, HD, CTX), BF16),
            pltpu.VMEM((NX, 8, CTX), F32),
            pltpu.VMEM((NX, HD, 512), BF16),
            pltpu.VMEM((NX, 8, 512), F32),
            pltpu.VMEM((NX, HD, 512), BF16),
            pltpu.VMEM((NX, 8, 512), F32),
            pltpu.VMEM((NX, 2, ROWS, 2 * HD), F32),
            pltpu.VMEM((NX, 2, ROWS, 2 * HD), F32),
            pltpu.VMEM((2, 2, ROWS, HD), F32),
            pltpu.VMEM((NX, 2, ROWS, HD), F32),
            pltpu.VMEM((CHUNKS // 2, CHUNK, PAGE, QCOLS), BF16),
            pltpu.VMEM((2, CHUNKS, CHUNK, PAGE, QCOLS), BF16),
            pltpu.VMEM((NX, FIN + 1, PAGE, QCOLS), BF16),
            pltpu.VMEM((QUARTERS, 2 * FIN, PAGE, QCOLS), BF16),
            pltpu.VMEM((8, 128), jnp.int32),
            pltpu.VMEM((NX, 8, 128), jnp.int32),
            pltpu.SMEM((NX, 8, 128), jnp.int32),
            dma((4,)),
            dma((NX,)),
            dma((NX,)),
            dma,
            dma((CHUNKS // 2,)),
            dma((2, CHUNKS)),
            dma((2, CHUNKS)),
        ]
        + [dma((NX,))] * 12
        + [dma((QUARTERS, NX)), dma((QUARTERS, NX)), dma((QUARTERS,))],
        compiler_params=pltpu.CompilerParams(
            collective_id=0, has_side_effects=True, vmem_limit_bytes=56 * 1024 * 1024
        ),
        cost_estimate=pl.CostEstimate(flops=4_500_000_000, bytes_accessed=12_000_000, transcendentals=8_500_000),
        name="attend_and_hand",
    )(
        queries[0],
        kv_cache.reshape(PAGES, PAGE, 2 * KVW),
        fresh_input[0],
        kv_weight,
        key_scale.reshape(1, KVW),
        ccos,
        csin,
        qcos,
        qsin,
        lengths.reshape(1),
        page_list,
        owners.reshape(FIN),
    )
    return attended, handed[None]


def solution(mesh):
    return jax.shard_map(
        shards,
        mesh=mesh,
        in_specs=(
            P(("sec", "grp"), None, None),
            P(("sec", "grp"), "rank", None),
            P(),
            P(("sec", "grp"), None, "rank"),
            P("rank", None),
            P(("sec", "grp"), None),
            P(("sec", "grp", "rank")),
            P(("sec", "grp", "rank"), None),
        ),
        out_specs=(P(("sec", "grp"), None, "rank"), P(("sec", "grp", "rank"), None, None, None)),
        check_vma=False,
    )
```

```python
import functools
import math

import jax
import jax.numpy as jnp
from jax import lax
from jax.experimental import pallas as pl
from jax.experimental.pallas import tpu as pltpu
from jax.sharding import PartitionSpec as P

HEADS = 64
KVH = 8
HD = 128
ROWS = 128
CTX = 1024
PAGE = 16
GQ = 8
KVW = 1024
PAGES = CTX // PAGE
FIN = 16
CAP = 2
NX = 4
RANKS = NX * NX
PARTS = 8
PCOLS = 2 * KVW // PARTS
WINDOW = 2
UNITS = KVH
WIDE = 512
SPAN = 64
BLOCKS = GQ * ROWS // WIDE
SEND_AT = ((1, 2), (2, 3), (4, 4), (5, 5), (6, 6), (7, 7))
DISPATCH_AT = ((3, 0), (5, 1), (7, 2))
FRESH_AT = 4

ROPE_BASE = 500000.0
NEG_FILL = -1e30
TO_LOG2 = math.log2(math.e) / math.sqrt(HD)

F32 = jnp.float32
BF16 = jnp.bfloat16
MESH = pl.DeviceIdType.MESH


def rope_tables(positions):
    half_width = HD // 2
    steps_index = jnp.arange(half_width, dtype=jnp.float32)
    inverse = jnp.exp(steps_index * (-2.0 * math.log(ROPE_BASE) / HD))
    angles = positions.astype(jnp.float32)[:, None] * inverse[None, :]
    return jnp.cos(angles), jnp.sin(angles)


def rotate(values, cosine, sine):
    swapped = pltpu.roll(values, HD // 2, 1)
    return values * cosine + swapped * sine


def dot_nt(a, b):
    return lax.dot_general(a, b, (((1,), (1,)), ((), ())), preferred_element_type=F32)


def soft_block(scores):
    peak = jnp.max(scores, axis=0, keepdims=True)
    weights = jnp.exp2(scores * TO_LOG2 - peak * TO_LOG2)
    total = jnp.sum(weights, axis=0, keepdims=True)
    return peak * TO_LOG2, total, weights.astype(BF16)


def merge(parts):
    top = functools.reduce(jnp.maximum, [p[0] for p in parts])
    factors = [jnp.exp2(p[0] - top) for p in parts]
    total = sum(p[1] * f for p, f in zip(parts, factors))
    numerator = sum(p[2] * f for p, f in zip(parts, factors))
    return top, total, numerator


def kernel(
    q_hbm, cache_hbm, fin_hbm, w_hbm, scale_ref, cos_half, sin_half, len_ref, plist_ref, own_ref,
    att_ref, handed_ref,
    q_ref, cache_ref, fin_ref, w_ref,
    keys, rows, vals_t, scores, weights, cos_ref, sin_ref,
    xs, xst, xr, xrt, zs, zst, zr, zrt,
    fs, fr, gs, gr,
    page_out, landed, work, picked, meta_out, meta_in, meta,
    load_sem, meta_send, meta_recv, meta_load, page_send, page_recv,
    xs_send, xs_recv, xt_send, xt_recv, zs_send, zs_recv, zt_send, zt_recv,
    f_send, f_recv, g_send, g_recv, pick_send, pick_recv, own_sem,
):
    sec, grp, rank = lax.axis_index("sec"), lax.axis_index("grp"), lax.axis_index("rank")
    x, z = lax.div(rank, NX), lax.rem(rank, NX)

    def at(xx, zz, section=None):
        return (sec if section is None else section, grp, xx * NX + zz)

    def remote(src, dst, send, recv, device):
        return pltpu.make_async_remote_copy(
            src_ref=src, dst_ref=dst, send_sem=send, recv_sem=recv, device_id=device, device_id_type=MESH
        )

    def plus(value, by):
        return lax.rem(value + by, NX)

    loads = [
        pltpu.make_async_copy(src, dst, load_sem.at[i])
        for i, (src, dst) in enumerate(
            ((cache_hbm, cache_ref), (fin_hbm, fin_ref), (w_hbm, w_ref), (q_hbm, q_ref))
        )
    ]
    for load in loads:
        load.start()

    barrier = pltpu.get_barrier_semaphore()
    for o in range(1, RANKS):
        peer = lax.rem(rank + o, RANKS)
        pl.semaphore_signal(barrier, inc=1, device_id=(sec, grp, peer), device_id_type=MESH)
    pl.semaphore_signal(barrier, inc=1, device_id=at(x, NX - 1 - z, 1 - sec), device_id_type=MESH)

    def page_copy(part):
        return remote(
            page_out.at[part], landed.at[part], page_send.at[part], page_recv.at[part], at(x, NX - 1 - z, 1)
        )

    def meta_copy():
        return remote(meta_out, meta_in, meta_send, meta_recv, at(x, NX - 1 - z, 1))

    loads[0].wait()

    @pl.when(sec == 0)
    def _():
        lanes = lax.broadcasted_iota(jnp.int32, (8, 128), 1)
        owner_of, slot_of = lanes // CAP, lanes % CAP
        count = jnp.zeros((8, 128), jnp.int32)
        chosen = jnp.full((8, 128), FIN, jnp.int32)
        for f in range(FIN):
            mine = owner_of == own_ref[f]
            chosen = jnp.where(mine & (count == slot_of), f, chosen)
            count = count + jnp.where(mine, 1, 0)
        meta_out[...] = chosen

        @pl.loop(0, FIN)
        def _(f):
            page = plist_ref[f]
            for part in range(PARTS):
                page_out[part, f] = cache_ref[page, :, part * PCOLS : (part + 1) * PCOLS]

    pl.semaphore_wait(barrier, RANKS)

    @pl.when(sec == 0)
    def _():
        meta_copy().start()
        for part in range(WINDOW):
            page_copy(part).start()

    loads[1].wait()
    loads[2].wait()

    def fresh_x(xx):
        o = plus(xx - x + NX, 0)
        return remote(fs.at[xx], fr.at[o], f_send.at[o], f_recv.at[o], at(xx, z))

    for xx in range(NX):
        for kind in range(2):
            cols = slice(kind * KVW + xx * 2 * HD, kind * KVW + (xx + 1) * 2 * HD)
            fs[xx, kind] = jnp.dot(fin_ref[...], w_ref[:, cols], preferred_element_type=F32)

        @pl.when(xx != x)
        def _():
            fresh_x(xx).start()

    def fresh_z(zz):
        o = plus(zz - z + NX, 0)
        return remote(gs.at[zz // 2], gr.at[o], g_send.at[o], g_recv.at[o], at(x, zz))

    def fresh_sum_x():
        for o in range(1, NX):
            remote(fs.at[0], fr.at[o], f_send.at[o], f_recv.at[o], at(plus(x, o), z)).wait_recv()
        for kind in range(2):
            total = fs[x, kind] + fr[1, kind] + fr[2, kind] + fr[3, kind]
            gs[0, kind] = total[:, :HD]
            gs[1, kind] = total[:, HD:]
        for zz in range(NX):

            @pl.when(zz != z)
            def _():
                fresh_z(zz).start()

    source = x * NX + NX - 1 - z

    def picked_copy(part, o):
        owner = lax.rem(rank + o, RANKS)
        return remote(
            picked.at[part, pl.ds(owner * CAP, CAP)],
            handed_ref.at[pl.ds(source * CAP, CAP), :, pl.ds(part * PCOLS, PCOLS)],
            pick_send.at[part, o],
            pick_recv.at[part, o],
            (1, grp, owner),
        )

    def picked_own(part):
        return pltpu.make_async_copy(
            picked.at[part, pl.ds(rank * CAP, CAP)],
            handed_ref.at[pl.ds(source * CAP, CAP), :, pl.ds(part * PCOLS, PCOLS)],
            own_sem.at[part],
        )

    def dispatch(part):
        if part == 0:
            meta_copy().wait_recv()
            load = pltpu.make_async_copy(meta_in, meta, meta_load)
            load.start()
            load.wait()
        page_copy(part).wait_recv()
        work[:FIN] = landed[part]
        for owner in range(RANKS):
            for c in range(CAP):
                picked[part, owner * CAP + c] = work[meta[0, owner * CAP + c]]

        @pl.loop(1, RANKS)
        def _(o):
            picked_copy(part, o).start()

        picked_own(part).start()

    def in_decode(*parts):
        @pl.when(sec == 1)
        def _():
            for part in parts:
                dispatch(part)

    @pl.when(sec == 1)
    def _():
        work[FIN] = jnp.zeros((PAGE, PCOLS), BF16)

    cos_ref[...] = jnp.concatenate([cos_half[...], cos_half[...]], axis=1)
    sin_ref[...] = jnp.concatenate([-sin_half[...], sin_half[...]], axis=1)
    loads[3].wait()
    edge = len_ref[0] - rank * CTX
    inside = lax.broadcasted_iota(jnp.int32, (CTX, HD), 0) < edge
    first = lax.broadcasted_iota(jnp.int32, (CTX, HD), 1) == 0
    keys[:, HD:] = jnp.where(first & jnp.logical_not(inside), NEG_FILL, 0.0).astype(BF16)
    rows[:, HD:] = jnp.where(first, 1.0, 0.0).astype(BF16)

    def xs_copy(o):
        xx = plus(x, o)
        return (
            remote(xs.at[xx], xr.at[o], xs_send.at[o], xs_recv.at[o], at(xx, z)),
            remote(xst.at[xx], xrt.at[o], xt_send.at[o], xt_recv.at[o], at(xx, z)),
        )

    @pl.loop(0, UNITS)
    def _(u):
        o = plus(lax.div(u, 2), 1)
        xx, hh = plus(x, o), lax.rem(u, 2)
        head = xx * 2 + hh
        cols = pl.ds(pl.multiple_of(head * HD, HD), HD)
        val_cols = pl.ds(pl.multiple_of(KVW + head * HD, HD), HD)
        for c in range(CTX // 128):
            span, pages = slice(c * 128, (c + 1) * 128), slice(c * 8, (c + 1) * 8)
            raw = cache_ref[pages, :, cols].reshape(128, HD).astype(F32) * scale_ref[:, cols]
            keys[span, :HD] = rotate(raw, cos_ref[span, :], sin_ref[span, :]).astype(BF16)
            vals_t[:, span] = cache_ref[pages, :, val_cols].reshape(128, HD).T
        for g in range(GQ):
            q_cols = pl.ds(pl.multiple_of((head * GQ + g) * HD, HD), HD)
            rows[g * ROWS : (g + 1) * ROWS, :HD] = rotate(
                q_ref[:, q_cols].astype(F32), cos_ref[CTX:, :], sin_ref[CTX:, :]
            ).astype(BF16)

        def score(b):
            scores[b] = dot_nt(keys[...], rows[b * WIDE : (b + 1) * WIDE, :])

        def weigh(b):
            peaks = scores[b, :SPAN].reshape(SPAN // 8, 8, WIDE).max(axis=0)
            for c in range(1, CTX // SPAN):
                part = scores[b, c * SPAN : (c + 1) * SPAN].reshape(SPAN // 8, 8, WIDE)
                peaks = jnp.maximum(peaks, part.max(axis=0))
            peak = peaks.max(axis=0, keepdims=True) * TO_LOG2
            base = jnp.broadcast_to(peak, (8, WIDE))
            totals = jnp.zeros((8, WIDE), F32)
            for c in range(CTX // SPAN):
                part = scores[b, c * SPAN : (c + 1) * SPAN].reshape(SPAN // 8, 8, WIDE)
                grown = jnp.exp2(part * TO_LOG2 - base[None])
                totals = totals + grown.sum(axis=0)
                weights[b, c * SPAN : (c + 1) * SPAN] = grown.reshape(SPAN, WIDE).astype(BF16)
            return peak, totals.sum(axis=0, keepdims=True)

        def add_up(b):
            numerator = jnp.dot(vals_t[...], weights[b], preferred_element_type=F32)
            xs[xx, hh, :, b * WIDE : (b + 1) * WIDE] = numerator.astype(BF16)

        stats = []
        score(0)
        for b in range(BLOCKS):
            if b + 1 < BLOCKS:
                score(b + 1)
            if b > 0:
                add_up(b - 1)
            stats.append(weigh(b))
        add_up(BLOCKS - 1)
        for h in range(2):

            @pl.when(hh == h)
            def _():
                for b in range(BLOCKS):
                    for i in range(2):
                        row = 2 * h + i
                        xst[xx, row : row + 1, b * WIDE : (b + 1) * WIDE] = stats[b][i]

        @pl.when((hh == 1) & (o != 0))
        def _():
            for copy in xs_copy(o):
                copy.start()

        for unit, part in SEND_AT:

            @pl.when((sec == 0) & (u == unit))
            def _():
                page_copy(part - WINDOW).wait_send()
                page_copy(part).start()

        for unit, part in DISPATCH_AT:

            @pl.when((sec == 1) & (u == unit))
            def _():
                dispatch(part)

        @pl.when(u == FRESH_AT)
        def _():
            fresh_sum_x()

    @pl.when(sec == 0)
    def _():
        picked[0] = jnp.zeros((RANKS * CAP, PAGE, PCOLS), BF16)
        for part in range(PARTS):
            pltpu.make_async_copy(
                picked.at[0], handed_ref.at[:, :, pl.ds(part * PCOLS, PCOLS)], own_sem.at[part]
            ).start()

    in_decode(3)

    for o in range(1, NX):
        for copy in xs_copy(o):
            copy.wait_recv()

    def zs_copy(zz):
        o = plus(zz - z + NX, 0)
        return (
            remote(zs.at[zz], zr.at[o], zs_send.at[o], zs_recv.at[o], at(x, zz)),
            remote(zst.at[zz], zrt.at[o], zt_send.at[o], zt_recv.at[o], at(x, zz)),
        )

    for zz in range(NX):
        hh, cols = zz // 2, slice((zz % 2) * 512, (zz % 2 + 1) * 512)
        parts = [
            (xst[x, 2 * hh : 2 * hh + 1, cols], xst[x, 2 * hh + 1 : 2 * hh + 2, cols], xs[x, hh, :, cols].astype(F32))
        ]
        for o in range(1, NX):
            parts.append(
                (
                    xrt[o, 2 * hh : 2 * hh + 1, cols],
                    xrt[o, 2 * hh + 1 : 2 * hh + 2, cols],
                    xr[o, hh, :, cols].astype(F32),
                )
            )
        top, total, numerator = merge(parts)
        zs[zz] = numerator.astype(BF16)
        zst[zz, 0:1, :] = top
        zst[zz, 1:2, :] = total

        @pl.when(zz != z)
        def _():
            for copy in zs_copy(zz):
                copy.start()

    in_decode(4, 5)

    for o in range(1, NX):
        remote(gs.at[0], gr.at[o], g_send.at[o], g_recv.at[o], at(x, plus(z, o))).wait_recv()
    mine = lax.div(z, 2)
    fresh = [(gs[mine, kind] + gr[1, kind] + gr[2, kind] + gr[3, kind]).astype(BF16) for kind in range(2)]
    fresh_keys = rotate(fresh[0].astype(F32), cos_ref[CTX:, :], sin_ref[CTX:, :]).astype(BF16)
    own_rows = []
    for h in range(HEADS // (NX * NX)):
        q_cols = pl.ds(pl.multiple_of((rank * 4 + h) * HD, HD), HD)
        own_rows.append(rotate(q_ref[:, q_cols].astype(F32), cos_ref[CTX:, :], sin_ref[CTX:, :]).astype(BF16))
    fresh_scores = dot_nt(fresh_keys, jnp.concatenate(own_rows, axis=0))
    key_row = lax.broadcasted_iota(jnp.int32, fresh_scores.shape, 0)
    query_row = lax.broadcasted_iota(jnp.int32, fresh_scores.shape, 1) % ROWS
    peak, total, fresh_weights = soft_block(jnp.where(key_row <= query_row, fresh_scores, NEG_FILL))
    numerator = jnp.dot(fresh[1].astype(F32).T.astype(BF16), fresh_weights, preferred_element_type=F32)
    parts = [(peak, total, numerator)]

    for o in range(1, NX):
        for copy in zs_copy(plus(z, o)):
            copy.wait_recv()
    parts.append((zst[z, 0:1, :], zst[z, 1:2, :], zs[z].astype(F32)))
    for o in range(1, NX):
        parts.append((zrt[o, 0:1, :], zrt[o, 1:2, :], zr[o].astype(F32)))
    _, total, numerator = merge(parts)
    result = numerator / total
    for h in range(HEADS // (NX * NX)):
        att_ref[0, :, h * HD : (h + 1) * HD] = result[:, h * ROWS : (h + 1) * ROWS].T.astype(BF16)

    in_decode(6, 7)

    for o in range(1, NX):
        for copy in xs_copy(o):
            copy.wait_send()
        for copy in zs_copy(plus(z, o)):
            copy.wait_send()
        fresh_x(plus(x, o)).wait_send()
        remote(gs.at[0], gr.at[o], g_send.at[o], g_recv.at[o], at(x, plus(z, o))).wait_send()

    @pl.when(sec == 0)
    def _():
        meta_copy().wait_send()
        for part in range(PARTS - WINDOW, PARTS):
            page_copy(part).wait_send()
        for part in range(PARTS):
            pltpu.make_async_copy(
                picked.at[0], handed_ref.at[:, :, pl.ds(part * PCOLS, PCOLS)], own_sem.at[part]
            ).wait()

    @pl.when(sec == 1)
    def _():
        for part in range(PARTS):

            @pl.loop(1, RANKS)
            def _(o):
                picked_copy(part, o).wait_send()
                picked_copy(part, o).wait_recv()

            picked_own(part).wait()


def shards(queries, kv_cache, key_scale, fresh_input, kv_weight, lengths, page_list, owners):
    position = lax.axis_index("rank")
    length = lengths[0, 0]
    places = jnp.arange(CTX + ROWS, dtype=jnp.int32)
    cosine, sine = rope_tables(jnp.where(places < CTX, position * CTX, length - CTX) + places)
    whole = pl.BlockSpec(memory_space=pltpu.VMEM)
    scalars = pl.BlockSpec(memory_space=pltpu.SMEM)
    anywhere = pl.BlockSpec(memory_space=pl.ANY)
    dma = pltpu.SemaphoreType.DMA
    attended, handed = pl.pallas_call(
        kernel,
        out_shape=(
            jax.ShapeDtypeStruct((1, ROWS, 512), BF16),
            jax.ShapeDtypeStruct((2 * FIN, PAGE, 2 * KVW), BF16),
        ),
        in_specs=[anywhere] * 4 + [whole] * 3 + [scalars] * 3,
        out_specs=(whole, anywhere),
        scratch_shapes=[
            pltpu.VMEM((ROWS, HEADS * HD), BF16),
            pltpu.VMEM((PAGES, PAGE, 2 * KVW), BF16),
            pltpu.VMEM((ROWS, 512), BF16),
            pltpu.VMEM((512, 2 * KVW), BF16),
            pltpu.VMEM((CTX, 2 * HD), BF16),
            pltpu.VMEM((CTX, 2 * HD), BF16),
            pltpu.VMEM((HD, CTX), BF16),
            pltpu.VMEM((BLOCKS, CTX, WIDE), F32),
            pltpu.VMEM((BLOCKS, CTX, WIDE), BF16),
            pltpu.VMEM((CTX + ROWS, HD), F32),
            pltpu.VMEM((CTX + ROWS, HD), F32),
            pltpu.VMEM((NX, 2, HD, CTX), BF16),
            pltpu.VMEM((NX, 8, CTX), F32),
            pltpu.VMEM((NX, 2, HD, CTX), BF16),
            pltpu.VMEM((NX, 8, CTX), F32),
            pltpu.VMEM((NX, HD, 512), BF16),
            pltpu.VMEM((NX, 8, 512), F32),
            pltpu.VMEM((NX, HD, 512), BF16),
            pltpu.VMEM((NX, 8, 512), F32),
            pltpu.VMEM((NX, 2, ROWS, 2 * HD), F32),
            pltpu.VMEM((NX, 2, ROWS, 2 * HD), F32),
            pltpu.VMEM((2, 2, ROWS, HD), F32),
            pltpu.VMEM((NX, 2, ROWS, HD), F32),
            pltpu.VMEM((PARTS, FIN, PAGE, PCOLS), BF16),
            pltpu.VMEM((PARTS, FIN, PAGE, PCOLS), BF16),
            pltpu.VMEM((FIN + 1, PAGE, PCOLS), BF16),
            pltpu.VMEM((PARTS, RANKS * CAP, PAGE, PCOLS), BF16),
            pltpu.VMEM((8, 128), jnp.int32),
            pltpu.VMEM((8, 128), jnp.int32),
            pltpu.SMEM((8, 128), jnp.int32),
            dma((4,)),
            dma,
            dma,
            dma,
            dma((PARTS,)),
            dma((PARTS,)),
        ]
        + [dma((NX,))] * 12
        + [dma((PARTS, RANKS)), dma((PARTS, RANKS)), dma((PARTS,))],
        compiler_params=pltpu.CompilerParams(
            collective_id=0, has_side_effects=True, vmem_limit_bytes=56 * 1024 * 1024
        ),
        cost_estimate=pl.CostEstimate(flops=4_500_000_000, bytes_accessed=12_000_000, transcendentals=8_500_000),
        name="attend_and_hand",
    )(
        queries[0],
        kv_cache.reshape(PAGES, PAGE, 2 * KVW),
        fresh_input[0],
        kv_weight,
        key_scale.reshape(1, KVW),
        cosine,
        sine,
        lengths.reshape(1),
        page_list,
        owners.reshape(FIN),
    )
    return attended, handed[None]


def solution(mesh):
    return jax.shard_map(
        shards,
        mesh=mesh,
        in_specs=(
            P(("sec", "grp"), None, None),
            P(("sec", "grp"), "rank", None),
            P(),
            P(("sec", "grp"), None, "rank"),
            P("rank", None),
            P(("sec", "grp"), None),
            P(("sec", "grp", "rank")),
            P(("sec", "grp", "rank"), None),
        ),
        out_specs=(P(("sec", "grp"), None, "rank"), P(("sec", "grp", "rank"), None, None, None)),
        check_vma=False,
    )
```

```python
import functools
import math

import jax
import jax.numpy as jnp
from jax import lax
from jax.experimental import pallas as pl
from jax.experimental.pallas import tpu as pltpu
from jax.sharding import PartitionSpec as P

HEADS = 64
KVH = 8
HD = 128
ROWS = 128
CTX = 1024
PAGE = 16
GQ = 8
KVW = 1024
PAGES = CTX // PAGE
FIN = 16
CAP = 2
NX = 4
RANKS = NX * NX
TABLE = CTX + ROWS
PARTS = 8
PCOLS = 2 * KVW // PARTS
WINDOW = 2
UNITS = KVH
WIDE = 512
SPAN = 64
BLOCKS = GQ * ROWS // WIDE
SEND_AT = ((1, 2), (2, 3), (4, 4), (5, 5), (6, 6), (7, 7))
DISPATCH_AT = ((1,0),(3,1),(5,2),(7,3))
FRESH_AT = 6

ROPE_BASE = 500000.0
NEG_FILL = -1e30
TO_LOG2 = math.log2(math.e) / math.sqrt(HD)

F32 = jnp.float32
BF16 = jnp.bfloat16
MESH = pl.DeviceIdType.MESH


def rope_tables(positions):
    half_width = HD // 2
    steps_index = jnp.arange(half_width, dtype=jnp.float32)
    inverse = jnp.exp(steps_index * (-2.0 * math.log(ROPE_BASE) / HD))
    angles = positions.astype(jnp.float32) * jnp.concatenate([inverse, inverse])[None, :]
    return jnp.cos(angles), jnp.sin(angles)


def rotate(values, cosine, sine):
    swapped = pltpu.roll(values, HD // 2, 1)
    return values * cosine + swapped * sine


def dot_nt(a, b):
    return lax.dot_general(a, b, (((1,), (1,)), ((), ())), preferred_element_type=F32)


def soft_block(scores):
    peak = jnp.max(scores, axis=0, keepdims=True)
    weights = jnp.exp2(scores * TO_LOG2 - peak * TO_LOG2)
    total = jnp.sum(weights, axis=0, keepdims=True)
    return peak * TO_LOG2, total, weights.astype(BF16)


def merge(parts):
    top = functools.reduce(jnp.maximum, [p[0] for p in parts])
    factors = [jnp.exp2(p[0] - top) for p in parts]
    total = sum(p[1] * f for p, f in zip(parts, factors))
    numerator = sum(p[2] * f for p, f in zip(parts, factors))
    return top, total, numerator


def kernel(
    q_hbm, cache_hbm, fin_hbm, w_hbm, scale_ref, cos_half, sin_half, len_ref, plist_ref, own_ref,
    att_ref, handed_ref,
    q_ref, cache_ref, fin_ref, w_ref,
    keys, rows, vals_t, scores, weights, cos_ref, sin_ref,
    xs, xst, xr, xrt, zs, zst, zr, zrt,
    fs, fr, gs, gr,
    page_out, landed, work, picked, meta_out, meta_in, meta,
    load_sem, meta_send, meta_recv, meta_load, page_send, page_recv,
    xs_send, xs_recv, xt_send, xt_recv, zs_send, zs_recv, zt_send, zt_recv,
    f_send, f_recv, g_send, g_recv, pick_send, pick_recv, own_sem,
):
    sec, grp, rank = lax.axis_index("sec"), lax.axis_index("grp"), lax.axis_index("rank")
    x, z = lax.div(rank, NX), lax.rem(rank, NX)

    def at(xx, zz, section=None):
        return (sec if section is None else section, grp, xx * NX + zz)

    def remote(src, dst, send, recv, device):
        return pltpu.make_async_remote_copy(
            src_ref=src, dst_ref=dst, send_sem=send, recv_sem=recv, device_id=device, device_id_type=MESH
        )

    def plus(value, by):
        return lax.rem(value + by, NX)

    loads = [
        pltpu.make_async_copy(src, dst, load_sem.at[i])
        for i, (src, dst) in enumerate(
            ((cache_hbm, cache_ref), (fin_hbm, fin_ref), (w_hbm, w_ref), (q_hbm, q_ref))
        )
    ]
    for load in loads:
        load.start()

    barrier = pltpu.get_barrier_semaphore()
    for o in range(1, RANKS):
        peer = lax.rem(rank + o, RANKS)
        pl.semaphore_signal(barrier, inc=1, device_id=(sec, grp, peer), device_id_type=MESH)
    pl.semaphore_signal(barrier, inc=1, device_id=at(x, NX - 1 - z, 1 - sec), device_id_type=MESH)

    def page_copy(part):
        return remote(
            page_out.at[part], landed.at[part], page_send.at[part], page_recv.at[part], at(x, NX - 1 - z, 1)
        )

    def meta_copy():
        return remote(meta_out, meta_in, meta_send, meta_recv, at(x, NX - 1 - z, 1))

    loads[0].wait()

    @pl.when(sec == 0)
    def _():
        lanes = lax.broadcasted_iota(jnp.int32, (8, 128), 1)
        owner_of, slot_of = lanes // CAP, lanes % CAP
        count = jnp.zeros((8, 128), jnp.int32)
        chosen = jnp.full((8, 128), FIN, jnp.int32)
        for f in range(FIN):
            mine = owner_of == own_ref[f]
            chosen = jnp.where(mine & (count == slot_of), f, chosen)
            count = count + jnp.where(mine, 1, 0)
        meta_out[...] = chosen

        @pl.loop(0, FIN)
        def _(f):
            page = plist_ref[f]
            for part in range(PARTS):
                page_out[part, f] = cache_ref[page, :, part * PCOLS : (part + 1) * PCOLS]

    pl.semaphore_wait(barrier, RANKS)

    @pl.when(sec == 0)
    def _():
        meta_copy().start()
        for part in range(WINDOW):
            page_copy(part).start()

    loads[1].wait()
    loads[2].wait()

    def fresh_x(xx):
        o = plus(xx - x + NX, 0)
        return remote(fs.at[xx], fr.at[o], f_send.at[o], f_recv.at[o], at(xx, z))

    for xx in range(NX):
        for kind in range(2):
            cols = slice(kind * KVW + xx * 2 * HD, kind * KVW + (xx + 1) * 2 * HD)
            fs[xx, kind] = jnp.dot(fin_ref[...], w_ref[:, cols], preferred_element_type=F32)

        @pl.when(xx != x)
        def _():
            fresh_x(xx).start()

    def fresh_z(zz):
        o = plus(zz - z + NX, 0)
        return remote(gs.at[zz // 2], gr.at[o], g_send.at[o], g_recv.at[o], at(x, zz))

    def fresh_sum_x():
        for o in range(1, NX):
            remote(fs.at[0], fr.at[o], f_send.at[o], f_recv.at[o], at(plus(x, o), z)).wait_recv()
        for kind in range(2):
            total = fs[x, kind] + fr[1, kind] + fr[2, kind] + fr[3, kind]
            gs[0, kind] = total[:, :HD]
            gs[1, kind] = total[:, HD:]
        for zz in range(NX):

            @pl.when(zz != z)
            def _():
                fresh_z(zz).start()

    source = x * NX + NX - 1 - z

    def picked_copy(part, o):
        owner = lax.rem(rank + o, RANKS)
        return remote(
            picked.at[part, pl.ds(owner * CAP, CAP)],
            handed_ref.at[pl.ds(source * CAP, CAP), :, pl.ds(part * PCOLS, PCOLS)],
            pick_send.at[part, o],
            pick_recv.at[part, o],
            (1, grp, owner),
        )

    def picked_own(part):
        return pltpu.make_async_copy(
            picked.at[part, pl.ds(rank * CAP, CAP)],
            handed_ref.at[pl.ds(source * CAP, CAP), :, pl.ds(part * PCOLS, PCOLS)],
            own_sem.at[part],
        )

    def dispatch(part):
        if part == 0:
            meta_copy().wait_recv()
            load = pltpu.make_async_copy(meta_in, meta, meta_load)
            load.start()
            load.wait()
        page_copy(part).wait_recv()
        work[:FIN] = landed[part]
        for owner in range(RANKS):
            for c in range(CAP):
                picked[part, owner * CAP + c] = work[meta[0, owner * CAP + c]]

        @pl.loop(1, RANKS)
        def _(o):
            picked_copy(part, o).start()

        picked_own(part).start()

    def in_decode(*parts):
        @pl.when(sec == 1)
        def _():
            for part in parts:
                dispatch(part)

    @pl.when(sec == 1)
    def _():
        work[FIN] = jnp.zeros((PAGE, PCOLS), BF16)

    low = lax.broadcasted_iota(jnp.int32, (TABLE // 2, HD), 1) < HD // 2
    cosine, sine = cos_half[...], sin_half[...]
    cosine_swapped, sine_swapped = pltpu.roll(cosine, HD // 2, 1), pltpu.roll(sine, HD // 2, 1)
    cos_ref[: TABLE // 2] = jnp.where(low, cosine, cosine_swapped)
    cos_ref[TABLE // 2 :] = jnp.where(low, cosine_swapped, cosine)
    sin_ref[: TABLE // 2] = jnp.where(low, -sine, sine_swapped)
    sin_ref[TABLE // 2 :] = jnp.where(low, -sine_swapped, sine)
    loads[3].wait()
    edge = len_ref[0] - rank * CTX
    inside = lax.broadcasted_iota(jnp.int32, (CTX, HD), 0) < edge
    first = lax.broadcasted_iota(jnp.int32, (CTX, HD), 1) == 0
    keys[:, HD:] = jnp.where(first & jnp.logical_not(inside), NEG_FILL, 0.0).astype(BF16)
    rows[:, HD:] = jnp.where(first, 1.0, 0.0).astype(BF16)

    def xs_copy(o):
        xx = plus(x, o)
        return (
            remote(xs.at[xx], xr.at[o], xs_send.at[o], xs_recv.at[o], at(xx, z)),
            remote(xst.at[xx], xrt.at[o], xt_send.at[o], xt_recv.at[o], at(xx, z)),
        )

    @pl.loop(0, UNITS)
    def _(u):
        o = plus(lax.div(u, 2), 1)
        xx, hh = plus(x, o), lax.rem(u, 2)
        head = xx * 2 + hh
        cols = pl.ds(pl.multiple_of(head * HD, HD), HD)
        val_cols = pl.ds(pl.multiple_of(KVW + head * HD, HD), HD)
        for c in range(CTX // 128):
            span, pages = slice(c * 128, (c + 1) * 128), slice(c * 8, (c + 1) * 8)
            raw = cache_ref[pages, :, cols].reshape(128, HD).astype(F32) * scale_ref[:, cols]
            keys[span, :HD] = rotate(raw, cos_ref[span, :], sin_ref[span, :]).astype(BF16)
            vals_t[:, span] = cache_ref[pages, :, val_cols].reshape(128, HD).T
        for g in range(GQ):
            q_cols = pl.ds(pl.multiple_of((head * GQ + g) * HD, HD), HD)
            rows[g * ROWS : (g + 1) * ROWS, :HD] = rotate(
                q_ref[:, q_cols].astype(F32), cos_ref[CTX:, :], sin_ref[CTX:, :]
            ).astype(BF16)

        def score(b):
            scores[b] = dot_nt(keys[...], rows[b * WIDE : (b + 1) * WIDE, :])

        def weigh(b):
            peaks = scores[b, :SPAN].reshape(SPAN // 8, 8, WIDE).max(axis=0)
            for c in range(1, CTX // SPAN):
                part = scores[b, c * SPAN : (c + 1) * SPAN].reshape(SPAN // 8, 8, WIDE)
                peaks = jnp.maximum(peaks, part.max(axis=0))
            peak = peaks.max(axis=0, keepdims=True) * TO_LOG2
            base = jnp.broadcast_to(peak, (8, WIDE))
            totals = jnp.zeros((8, WIDE), F32)
            for c in range(CTX // SPAN):
                part = scores[b, c * SPAN : (c + 1) * SPAN].reshape(SPAN // 8, 8, WIDE)
                grown = jnp.exp2(part * TO_LOG2 - base[None])
                totals = totals + grown.sum(axis=0)
                weights[b, c * SPAN : (c + 1) * SPAN] = grown.reshape(SPAN, WIDE).astype(BF16)
            return peak, totals.sum(axis=0, keepdims=True)

        def add_up(b):
            numerator = jnp.dot(vals_t[...], weights[b], preferred_element_type=F32)
            xs[xx, hh, :, b * WIDE : (b + 1) * WIDE] = numerator.astype(BF16)

        stats = []
        score(0)
        for b in range(BLOCKS):
            if b + 1 < BLOCKS:
                score(b + 1)
            if b > 0:
                add_up(b - 1)
            stats.append(weigh(b))
        add_up(BLOCKS - 1)
        for h in range(2):

            @pl.when(hh == h)
            def _():
                for b in range(BLOCKS):
                    for i in range(2):
                        row = 2 * h + i
                        xst[xx, row : row + 1, b * WIDE : (b + 1) * WIDE] = stats[b][i]

        @pl.when((hh == 1) & (o != 0))
        def _():
            for copy in xs_copy(o):
                copy.start()

        for unit, part in SEND_AT:

            @pl.when((sec == 0) & (u == unit))
            def _():
                page_copy(part - WINDOW).wait_send()
                page_copy(part).start()

        for unit, part in DISPATCH_AT:

            @pl.when((sec == 1) & (u == unit))
            def _():
                dispatch(part)

        @pl.when(u == FRESH_AT)
        def _():
            fresh_sum_x()

    @pl.when(sec == 0)
    def _():
        picked[0] = jnp.zeros((RANKS * CAP, PAGE, PCOLS), BF16)
        for part in range(PARTS):
            pltpu.make_async_copy(
                picked.at[0], handed_ref.at[:, :, pl.ds(part * PCOLS, PCOLS)], own_sem.at[part]
            ).start()

    in_decode(4, 5, 6)

    for o in range(1, NX):
        for copy in xs_copy(o):
            copy.wait_recv()

    def zs_copy(zz):
        o = plus(zz - z + NX, 0)
        return (
            remote(zs.at[zz], zr.at[o], zs_send.at[o], zs_recv.at[o], at(x, zz)),
            remote(zst.at[zz], zrt.at[o], zt_send.at[o], zt_recv.at[o], at(x, zz)),
        )

    for zz in range(NX):
        hh, cols = zz // 2, slice((zz % 2) * 512, (zz % 2 + 1) * 512)
        parts = [
            (xst[x, 2 * hh : 2 * hh + 1, cols], xst[x, 2 * hh + 1 : 2 * hh + 2, cols], xs[x, hh, :, cols].astype(F32))
        ]
        for o in range(1, NX):
            parts.append(
                (
                    xrt[o, 2 * hh : 2 * hh + 1, cols],
                    xrt[o, 2 * hh + 1 : 2 * hh + 2, cols],
                    xr[o, hh, :, cols].astype(F32),
                )
            )
        top, total, numerator = merge(parts)
        zs[zz] = numerator.astype(BF16)
        zst[zz, 0:1, :] = top
        zst[zz, 1:2, :] = total

        @pl.when(zz != z)
        def _():
            for copy in zs_copy(zz):
                copy.start()


    for o in range(1, NX):
        remote(gs.at[0], gr.at[o], g_send.at[o], g_recv.at[o], at(x, plus(z, o))).wait_recv()
    mine = lax.div(z, 2)
    fresh = [(gs[mine, kind] + gr[1, kind] + gr[2, kind] + gr[3, kind]).astype(BF16) for kind in range(2)]
    fresh_keys = rotate(fresh[0].astype(F32), cos_ref[CTX:, :], sin_ref[CTX:, :]).astype(BF16)
    own_rows = []
    for h in range(HEADS // (NX * NX)):
        q_cols = pl.ds(pl.multiple_of((rank * 4 + h) * HD, HD), HD)
        own_rows.append(rotate(q_ref[:, q_cols].astype(F32), cos_ref[CTX:, :], sin_ref[CTX:, :]).astype(BF16))
    fresh_scores = dot_nt(fresh_keys, jnp.concatenate(own_rows, axis=0))
    key_row = lax.broadcasted_iota(jnp.int32, fresh_scores.shape, 0)
    query_row = lax.broadcasted_iota(jnp.int32, fresh_scores.shape, 1) % ROWS
    peak, total, fresh_weights = soft_block(jnp.where(key_row <= query_row, fresh_scores, NEG_FILL))
    numerator = jnp.dot(fresh[1].astype(F32).T.astype(BF16), fresh_weights, preferred_element_type=F32)
    parts = [(peak, total, numerator)]

    in_decode(7)

    for o in range(1, NX):
        for copy in zs_copy(plus(z, o)):
            copy.wait_recv()
    parts.append((zst[z, 0:1, :], zst[z, 1:2, :], zs[z].astype(F32)))
    for o in range(1, NX):
        parts.append((zrt[o, 0:1, :], zrt[o, 1:2, :], zr[o].astype(F32)))
    _, total, numerator = merge(parts)
    result = numerator / total
    for h in range(HEADS // (NX * NX)):
        att_ref[0, :, h * HD : (h + 1) * HD] = result[:, h * ROWS : (h + 1) * ROWS].T.astype(BF16)

    for o in range(1, NX):
        for copy in xs_copy(o):
            copy.wait_send()
        for copy in zs_copy(plus(z, o)):
            copy.wait_send()
        fresh_x(plus(x, o)).wait_send()
        remote(gs.at[0], gr.at[o], g_send.at[o], g_recv.at[o], at(x, plus(z, o))).wait_send()

    @pl.when(sec == 0)
    def _():
        meta_copy().wait_send()
        for part in range(PARTS - WINDOW, PARTS):
            page_copy(part).wait_send()
        for part in range(PARTS):
            pltpu.make_async_copy(
                picked.at[0], handed_ref.at[:, :, pl.ds(part * PCOLS, PCOLS)], own_sem.at[part]
            ).wait()

    @pl.when(sec == 1)
    def _():
        for part in range(PARTS):

            @pl.loop(1, RANKS)
            def _(o):
                picked_copy(part, o).wait_send()
                picked_copy(part, o).wait_recv()

            picked_own(part).wait()


def place_kernel(att_in, handed_in, att_out, handed_out):
    att_out[...] = att_in[...]
    handed_out[0] = handed_in[...]


def shards(queries, kv_cache, key_scale, fresh_input, kv_weight, lengths, page_list, owners):
    position = lax.axis_index("rank")
    length = lengths[0, 0]
    places = lax.broadcasted_iota(jnp.int32, (TABLE // 2, HD), 0)
    lanes = lax.broadcasted_iota(jnp.int32, (TABLE // 2, HD), 1)
    places = places + jnp.where(lanes < HD // 2, 0, TABLE // 2)
    cosine, sine = rope_tables(jnp.where(places < CTX, position * CTX, length - CTX) + places)
    whole = pl.BlockSpec(memory_space=pltpu.VMEM)
    scalars = pl.BlockSpec(memory_space=pltpu.SMEM)
    anywhere = pl.BlockSpec(memory_space=pl.ANY)
    dma = pltpu.SemaphoreType.DMA
    attended, handed = pl.pallas_call(
        kernel,
        out_shape=(
            jax.ShapeDtypeStruct((1, ROWS, 512), BF16),
            jax.ShapeDtypeStruct((2 * FIN, PAGE, 2 * KVW), BF16),
        ),
        in_specs=[anywhere] * 4 + [whole] * 3 + [scalars] * 3,
        out_specs=(whole, anywhere),
        scratch_shapes=[
            pltpu.VMEM((ROWS, HEADS * HD), BF16),
            pltpu.VMEM((PAGES, PAGE, 2 * KVW), BF16),
            pltpu.VMEM((ROWS, 512), BF16),
            pltpu.VMEM((512, 2 * KVW), BF16),
            pltpu.VMEM((CTX, 2 * HD), BF16),
            pltpu.VMEM((CTX, 2 * HD), BF16),
            pltpu.VMEM((HD, CTX), BF16),
            pltpu.VMEM((BLOCKS, CTX, WIDE), F32),
            pltpu.VMEM((BLOCKS, CTX, WIDE), BF16),
            pltpu.VMEM((CTX + ROWS, HD), F32),
            pltpu.VMEM((CTX + ROWS, HD), F32),
            pltpu.VMEM((NX, 2, HD, CTX), BF16),
            pltpu.VMEM((NX, 8, CTX), F32),
            pltpu.VMEM((NX, 2, HD, CTX), BF16),
            pltpu.VMEM((NX, 8, CTX), F32),
            pltpu.VMEM((NX, HD, 512), BF16),
            pltpu.VMEM((NX, 8, 512), F32),
            pltpu.VMEM((NX, HD, 512), BF16),
            pltpu.VMEM((NX, 8, 512), F32),
            pltpu.VMEM((NX, 2, ROWS, 2 * HD), F32),
            pltpu.VMEM((NX, 2, ROWS, 2 * HD), F32),
            pltpu.VMEM((2, 2, ROWS, HD), F32),
            pltpu.VMEM((NX, 2, ROWS, HD), F32),
            pltpu.VMEM((PARTS, FIN, PAGE, PCOLS), BF16),
            pltpu.VMEM((PARTS, FIN, PAGE, PCOLS), BF16),
            pltpu.VMEM((FIN + 1, PAGE, PCOLS), BF16),
            pltpu.VMEM((PARTS, RANKS * CAP, PAGE, PCOLS), BF16),
            pltpu.VMEM((8, 128), jnp.int32),
            pltpu.VMEM((8, 128), jnp.int32),
            pltpu.SMEM((8, 128), jnp.int32),
            dma((4,)),
            dma,
            dma,
            dma,
            dma((PARTS,)),
            dma((PARTS,)),
        ]
        + [dma((NX,))] * 12
        + [dma((PARTS, RANKS)), dma((PARTS, RANKS)), dma((PARTS,))],
        compiler_params=pltpu.CompilerParams(
            collective_id=0, has_side_effects=True, vmem_limit_bytes=56 * 1024 * 1024
        ),
        cost_estimate=pl.CostEstimate(flops=4_500_000_000, bytes_accessed=12_000_000, transcendentals=8_500_000),
        name="attend_and_hand",
    )(
        queries[0],
        kv_cache.reshape(PAGES, PAGE, 2 * KVW),
        fresh_input[0],
        kv_weight,
        key_scale.reshape(1, KVW),
        cosine,
        sine,
        lengths.reshape(1),
        page_list,
        owners.reshape(FIN),
    )
    return pl.pallas_call(
        place_kernel,
        out_shape=(
            jax.ShapeDtypeStruct((1, ROWS, 512), BF16),
            jax.ShapeDtypeStruct((1, 2 * FIN, PAGE, 2 * KVW), BF16),
        ),
        in_specs=[whole] * 2,
        out_specs=(whole, whole),

        cost_estimate=pl.CostEstimate(flops=0, bytes_accessed=4_500_000, transcendentals=0),
        name="place",
    )(attended, handed)


def solution(mesh):
    return jax.shard_map(
        shards,
        mesh=mesh,
        in_specs=(
            P(("sec", "grp"), None, None),
            P(("sec", "grp"), "rank", None),
            P(),
            P(("sec", "grp"), None, "rank"),
            P("rank", None),
            P(("sec", "grp"), None),
            P(("sec", "grp", "rank")),
            P(("sec", "grp", "rank"), None),
        ),
        out_specs=(P(("sec", "grp"), None, "rank"), P(("sec", "grp", "rank"), None, None, None)),
        check_vma=False,
    )
```

```python
import functools
import math

import jax
import jax.numpy as jnp
from jax import lax
from jax.experimental import pallas as pl
from jax.experimental.pallas import tpu as pltpu
from jax.sharding import PartitionSpec as P

HEADS = 64
KVH = 8
HD = 128
ROWS = 128
CTX = 1024
PAGE = 16
GQ = 8
KVW = 1024
PAGES = CTX // PAGE
FIN = 16
CAP = 2
NX = 4
RANKS = NX * NX
TABLE = CTX + ROWS
PARTS = 8
PCOLS = 2 * KVW // PARTS
WINDOW = 2
UNITS = KVH
WIDE = 512
SPAN = 64
BLOCKS = GQ * ROWS // WIDE
SEND_AT = ((1, 2), (2, 3), (4, 4), (5, 5), (6, 6), (7, 7))
DISPATCH_AT = ((1,0),(3,1),(5,2),(7,3))
FRESH_AT = 6

ROPE_BASE = 500000.0
NEG_FILL = -1e30
TO_LOG2 = math.log2(math.e) / math.sqrt(HD)

F32 = jnp.float32
BF16 = jnp.bfloat16
MESH = pl.DeviceIdType.MESH


def rope_tables(positions):
    half_width = HD // 2
    steps_index = jnp.arange(half_width, dtype=jnp.float32)
    inverse = jnp.exp(steps_index * (-2.0 * math.log(ROPE_BASE) / HD))
    angles = positions.astype(jnp.float32) * jnp.concatenate([inverse, inverse])[None, :]
    return jnp.cos(angles), jnp.sin(angles)


def rotate(values, cosine, sine):
    swapped = pltpu.roll(values, HD // 2, 1)
    return values * cosine + swapped * sine


def dot_nt(a, b):
    return lax.dot_general(a, b, (((1,), (1,)), ((), ())), preferred_element_type=F32)


def soft_block(scores):
    peak = jnp.max(scores, axis=0, keepdims=True)
    weights = jnp.exp2(scores * TO_LOG2 - peak * TO_LOG2)
    total = jnp.sum(weights, axis=0, keepdims=True)
    return peak * TO_LOG2, total, weights.astype(BF16)


def merge(parts):
    top = functools.reduce(jnp.maximum, [p[0] for p in parts])
    factors = [jnp.exp2(p[0] - top) for p in parts]
    total = sum(p[1] * f for p, f in zip(parts, factors))
    numerator = sum(p[2] * f for p, f in zip(parts, factors))
    return top, total, numerator


def kernel(
    q_hbm, cache_hbm, fin_hbm, w_hbm, scale_ref, cos_half, sin_half, len_ref, plist_ref, own_ref,
    att_ref, handed_ref,
    q_ref, cache_ref, fin_ref, w_ref,
    keys, rows, vals_t, scores, weights, cos_ref, sin_ref,
    xs, xst, xr, xrt, zs, zst, zr, zrt,
    fs, fr, gs, gr,
    page_out, landed, work, picked, meta_out, meta_in, meta,
    load_sem, meta_send, meta_recv, meta_load, page_send, page_recv,
    xs_send, xs_recv, xt_send, xt_recv, zs_send, zs_recv, zt_send, zt_recv,
    f_send, f_recv, g_send, g_recv, pick_send, pick_recv, own_sem,
):
    sec, grp, rank = lax.axis_index("sec"), lax.axis_index("grp"), lax.axis_index("rank")
    x, z = lax.div(rank, NX), lax.rem(rank, NX)

    def at(xx, zz, section=None):
        return (sec if section is None else section, grp, xx * NX + zz)

    def remote(src, dst, send, recv, device):
        return pltpu.make_async_remote_copy(
            src_ref=src, dst_ref=dst, send_sem=send, recv_sem=recv, device_id=device, device_id_type=MESH
        )

    def plus(value, by):
        return lax.rem(value + by, NX)

    loads = [
        pltpu.make_async_copy(src, dst, load_sem.at[i])
        for i, (src, dst) in enumerate(
            ((cache_hbm, cache_ref), (fin_hbm, fin_ref), (w_hbm, w_ref), (q_hbm, q_ref))
        )
    ]
    for load in loads:
        load.start()

    barrier = pltpu.get_barrier_semaphore()
    for o in range(1, RANKS):
        peer = lax.rem(rank + o, RANKS)
        pl.semaphore_signal(barrier, inc=1, device_id=(sec, grp, peer), device_id_type=MESH)
    pl.semaphore_signal(barrier, inc=1, device_id=at(x, NX - 1 - z, 1 - sec), device_id_type=MESH)

    def page_copy(part):
        return remote(
            page_out.at[part], landed.at[part], page_send.at[part], page_recv.at[part], at(x, NX - 1 - z, 1)
        )

    def meta_copy():
        return remote(meta_out, meta_in, meta_send, meta_recv, at(x, NX - 1 - z, 1))

    loads[0].wait()

    @pl.when(sec == 0)
    def _():
        lanes = lax.broadcasted_iota(jnp.int32, (8, 128), 1)
        owner_of, slot_of = lanes // CAP, lanes % CAP
        count = jnp.zeros((8, 128), jnp.int32)
        chosen = jnp.full((8, 128), FIN, jnp.int32)
        for f in range(FIN):
            mine = owner_of == own_ref[f]
            chosen = jnp.where(mine & (count == slot_of), f, chosen)
            count = count + jnp.where(mine, 1, 0)
        meta_out[...] = chosen

        @pl.loop(0, FIN)
        def _(f):
            page = plist_ref[f]
            for part in range(PARTS):
                page_out[part, f] = cache_ref[page, :, part * PCOLS : (part + 1) * PCOLS]

    loads[1].wait()
    loads[2].wait()

    def fresh_x(xx):
        o = plus(xx - x + NX, 0)
        return remote(fs.at[xx], fr.at[o], f_send.at[o], f_recv.at[o], at(xx, z))

    for xx in range(NX):
        for kind in range(2):
            cols = slice(kind * KVW + xx * 2 * HD, kind * KVW + (xx + 1) * 2 * HD)
            fs[xx, kind] = jnp.dot(fin_ref[...], w_ref[:, cols], preferred_element_type=F32)

    low = lax.broadcasted_iota(jnp.int32, (TABLE // 2, HD), 1) < HD // 2
    cosine, sine = cos_half[...], sin_half[...]
    cosine_swapped, sine_swapped = pltpu.roll(cosine, HD // 2, 1), pltpu.roll(sine, HD // 2, 1)
    cos_ref[: TABLE // 2] = jnp.where(low, cosine, cosine_swapped)
    cos_ref[TABLE // 2 :] = jnp.where(low, cosine_swapped, cosine)
    sin_ref[: TABLE // 2] = jnp.where(low, -sine, sine_swapped)
    sin_ref[TABLE // 2 :] = jnp.where(low, -sine_swapped, sine)
    loads[3].wait()
    pl.semaphore_wait(barrier, RANKS)

    @pl.when(sec == 0)
    def _():
        meta_copy().start()
        for part in range(WINDOW):
            page_copy(part).start()

    for xx in range(NX):

        @pl.when(xx != x)
        def _():
            fresh_x(xx).start()

    def fresh_z(zz):
        o = plus(zz - z + NX, 0)
        return remote(gs.at[zz // 2], gr.at[o], g_send.at[o], g_recv.at[o], at(x, zz))

    def fresh_sum_x():
        for o in range(1, NX):
            remote(fs.at[0], fr.at[o], f_send.at[o], f_recv.at[o], at(plus(x, o), z)).wait_recv()
        for kind in range(2):
            total = fs[x, kind] + fr[1, kind] + fr[2, kind] + fr[3, kind]
            gs[0, kind] = total[:, :HD]
            gs[1, kind] = total[:, HD:]
        for zz in range(NX):

            @pl.when(zz != z)
            def _():
                fresh_z(zz).start()

    source = x * NX + NX - 1 - z

    def picked_copy(part, o):
        owner = lax.rem(rank + o, RANKS)
        return remote(
            picked.at[part, pl.ds(owner * CAP, CAP)],
            handed_ref.at[pl.ds(source * CAP, CAP), :, pl.ds(part * PCOLS, PCOLS)],
            pick_send.at[part, o],
            pick_recv.at[part, o],
            (1, grp, owner),
        )

    def picked_own(part):
        return pltpu.make_async_copy(
            picked.at[part, pl.ds(rank * CAP, CAP)],
            handed_ref.at[pl.ds(source * CAP, CAP), :, pl.ds(part * PCOLS, PCOLS)],
            own_sem.at[part],
        )

    def dispatch(part):
        if part == 0:
            meta_copy().wait_recv()
            load = pltpu.make_async_copy(meta_in, meta, meta_load)
            load.start()
            load.wait()
        page_copy(part).wait_recv()
        work[:FIN] = landed[part]
        for owner in range(RANKS):
            for c in range(CAP):
                picked[part, owner * CAP + c] = work[meta[0, owner * CAP + c]]

        @pl.loop(1, RANKS)
        def _(o):
            picked_copy(part, o).start()

        picked_own(part).start()

    def in_decode(*parts):
        @pl.when(sec == 1)
        def _():
            for part in parts:
                dispatch(part)

    @pl.when(sec == 1)
    def _():
        work[FIN] = jnp.zeros((PAGE, PCOLS), BF16)

    edge = len_ref[0] - rank * CTX
    inside = lax.broadcasted_iota(jnp.int32, (CTX, HD), 0) < edge
    first = lax.broadcasted_iota(jnp.int32, (CTX, HD), 1) == 0
    keys[:, HD:] = jnp.where(first & jnp.logical_not(inside), NEG_FILL, 0.0).astype(BF16)
    rows[:, HD:] = jnp.where(first, 1.0, 0.0).astype(BF16)

    def xs_copy(o):
        xx = plus(x, o)
        return (
            remote(xs.at[xx], xr.at[o], xs_send.at[o], xs_recv.at[o], at(xx, z)),
            remote(xst.at[xx], xrt.at[o], xt_send.at[o], xt_recv.at[o], at(xx, z)),
        )

    @pl.loop(0, UNITS)
    def _(u):
        o = plus(lax.div(u, 2), 1)
        xx, hh = plus(x, o), lax.rem(u, 2)
        head = xx * 2 + hh
        cols = pl.ds(pl.multiple_of(head * HD, HD), HD)
        val_cols = pl.ds(pl.multiple_of(KVW + head * HD, HD), HD)
        for c in range(CTX // 128):
            span, pages = slice(c * 128, (c + 1) * 128), slice(c * 8, (c + 1) * 8)
            raw = cache_ref[pages, :, cols].reshape(128, HD).astype(F32) * scale_ref[:, cols]
            keys[span, :HD] = rotate(raw, cos_ref[span, :], sin_ref[span, :]).astype(BF16)
            vals_t[:, span] = cache_ref[pages, :, val_cols].reshape(128, HD).T
        for g in range(GQ):
            q_cols = pl.ds(pl.multiple_of((head * GQ + g) * HD, HD), HD)
            rows[g * ROWS : (g + 1) * ROWS, :HD] = rotate(
                q_ref[:, q_cols].astype(F32), cos_ref[CTX:, :], sin_ref[CTX:, :]
            ).astype(BF16)

        def score(b):
            scores[b] = dot_nt(keys[...], rows[b * WIDE : (b + 1) * WIDE, :])

        def weigh(b):
            peaks = scores[b, :SPAN].reshape(SPAN // 8, 8, WIDE).max(axis=0)
            for c in range(1, CTX // SPAN):
                part = scores[b, c * SPAN : (c + 1) * SPAN].reshape(SPAN // 8, 8, WIDE)
                peaks = jnp.maximum(peaks, part.max(axis=0))
            peak = peaks.max(axis=0, keepdims=True) * TO_LOG2
            base = jnp.broadcast_to(peak, (8, WIDE))
            totals = jnp.zeros((8, WIDE), F32)
            for c in range(CTX // SPAN):
                part = scores[b, c * SPAN : (c + 1) * SPAN].reshape(SPAN // 8, 8, WIDE)
                grown = jnp.exp2(part * TO_LOG2 - base[None])
                totals = totals + grown.sum(axis=0)
                weights[b, c * SPAN : (c + 1) * SPAN] = grown.reshape(SPAN, WIDE).astype(BF16)
            return peak, totals.sum(axis=0, keepdims=True)

        def add_up(b):
            numerator = jnp.dot(vals_t[...], weights[b], preferred_element_type=F32)
            xs[xx, hh, :, b * WIDE : (b + 1) * WIDE] = numerator.astype(BF16)

        stats = []
        score(0)
        for b in range(BLOCKS):
            if b + 1 < BLOCKS:
                score(b + 1)
            if b > 0:
                add_up(b - 1)
            stats.append(weigh(b))
        add_up(BLOCKS - 1)
        for h in range(2):

            @pl.when(hh == h)
            def _():
                for b in range(BLOCKS):
                    for i in range(2):
                        row = 2 * h + i
                        xst[xx, row : row + 1, b * WIDE : (b + 1) * WIDE] = stats[b][i]

        @pl.when((hh == 1) & (o != 0))
        def _():
            for copy in xs_copy(o):
                copy.start()

        for unit, part in SEND_AT:

            @pl.when((sec == 0) & (u == unit))
            def _():
                page_copy(part - WINDOW).wait_send()
                page_copy(part).start()

        for unit, part in DISPATCH_AT:

            @pl.when((sec == 1) & (u == unit))
            def _():
                dispatch(part)

        @pl.when(u == FRESH_AT)
        def _():
            fresh_sum_x()

    @pl.when(sec == 0)
    def _():
        picked[0] = jnp.zeros((RANKS * CAP, PAGE, PCOLS), BF16)
        for part in range(PARTS):
            pltpu.make_async_copy(
                picked.at[0], handed_ref.at[:, :, pl.ds(part * PCOLS, PCOLS)], own_sem.at[part]
            ).start()

    in_decode(4, 5, 6, 7)

    for o in range(1, NX):
        for copy in xs_copy(o):
            copy.wait_recv()

    def zs_copy(zz):
        o = plus(zz - z + NX, 0)
        return (
            remote(zs.at[zz], zr.at[o], zs_send.at[o], zs_recv.at[o], at(x, zz)),
            remote(zst.at[zz], zrt.at[o], zt_send.at[o], zt_recv.at[o], at(x, zz)),
        )

    for zz in range(NX):
        hh, cols = zz // 2, slice((zz % 2) * 512, (zz % 2 + 1) * 512)
        parts = [
            (xst[x, 2 * hh : 2 * hh + 1, cols], xst[x, 2 * hh + 1 : 2 * hh + 2, cols], xs[x, hh, :, cols].astype(F32))
        ]
        for o in range(1, NX):
            parts.append(
                (
                    xrt[o, 2 * hh : 2 * hh + 1, cols],
                    xrt[o, 2 * hh + 1 : 2 * hh + 2, cols],
                    xr[o, hh, :, cols].astype(F32),
                )
            )
        top, total, numerator = merge(parts)
        zs[zz] = numerator.astype(BF16)
        zst[zz, 0:1, :] = top
        zst[zz, 1:2, :] = total

        @pl.when(zz != z)
        def _():
            for copy in zs_copy(zz):
                copy.start()


    for o in range(1, NX):
        remote(gs.at[0], gr.at[o], g_send.at[o], g_recv.at[o], at(x, plus(z, o))).wait_recv()
    mine = lax.div(z, 2)
    fresh = [(gs[mine, kind] + gr[1, kind] + gr[2, kind] + gr[3, kind]).astype(BF16) for kind in range(2)]
    fresh_keys = rotate(fresh[0].astype(F32), cos_ref[CTX:, :], sin_ref[CTX:, :]).astype(BF16)
    own_rows = []
    for h in range(HEADS // (NX * NX)):
        q_cols = pl.ds(pl.multiple_of((rank * 4 + h) * HD, HD), HD)
        own_rows.append(rotate(q_ref[:, q_cols].astype(F32), cos_ref[CTX:, :], sin_ref[CTX:, :]).astype(BF16))
    fresh_scores = dot_nt(fresh_keys, jnp.concatenate(own_rows, axis=0))
    key_row = lax.broadcasted_iota(jnp.int32, fresh_scores.shape, 0)
    query_row = lax.broadcasted_iota(jnp.int32, fresh_scores.shape, 1) % ROWS
    peak, total, fresh_weights = soft_block(jnp.where(key_row <= query_row, fresh_scores, NEG_FILL))
    numerator = jnp.dot(fresh[1].astype(F32).T.astype(BF16), fresh_weights, preferred_element_type=F32)
    parts = [(peak, total, numerator)]

    for o in range(1, NX):
        for copy in zs_copy(plus(z, o)):
            copy.wait_recv()
    parts.append((zst[z, 0:1, :], zst[z, 1:2, :], zs[z].astype(F32)))
    for o in range(1, NX):
        parts.append((zrt[o, 0:1, :], zrt[o, 1:2, :], zr[o].astype(F32)))
    _, total, numerator = merge(parts)
    result = numerator / total
    for h in range(HEADS // (NX * NX)):
        att_ref[0, :, h * HD : (h + 1) * HD] = result[:, h * ROWS : (h + 1) * ROWS].T.astype(BF16)

    for o in range(1, NX):
        for copy in xs_copy(o):
            copy.wait_send()
        for copy in zs_copy(plus(z, o)):
            copy.wait_send()
        fresh_x(plus(x, o)).wait_send()
        remote(gs.at[0], gr.at[o], g_send.at[o], g_recv.at[o], at(x, plus(z, o))).wait_send()

    @pl.when(sec == 0)
    def _():
        meta_copy().wait_send()
        for part in range(PARTS - WINDOW, PARTS):
            page_copy(part).wait_send()
        for part in range(PARTS):
            pltpu.make_async_copy(
                picked.at[0], handed_ref.at[:, :, pl.ds(part * PCOLS, PCOLS)], own_sem.at[part]
            ).wait()

    @pl.when(sec == 1)
    def _():
        for part in range(PARTS):

            @pl.loop(1, RANKS)
            def _(o):
                picked_copy(part, o).wait_send()
                picked_copy(part, o).wait_recv()

            picked_own(part).wait()


def place_kernel(att_in, handed_in, att_out, handed_out):
    att_out[...] = att_in[...]
    handed_out[0] = handed_in[...]


def shards(queries, kv_cache, key_scale, fresh_input, kv_weight, lengths, page_list, owners):
    position = lax.axis_index("rank")
    length = lengths[0, 0]
    places = lax.broadcasted_iota(jnp.int32, (TABLE // 2, HD), 0)
    lanes = lax.broadcasted_iota(jnp.int32, (TABLE // 2, HD), 1)
    places = places + jnp.where(lanes < HD // 2, 0, TABLE // 2)
    cosine, sine = rope_tables(jnp.where(places < CTX, position * CTX, length - CTX) + places)
    whole = pl.BlockSpec(memory_space=pltpu.VMEM)
    scalars = pl.BlockSpec(memory_space=pltpu.SMEM)
    anywhere = pl.BlockSpec(memory_space=pl.ANY)
    dma = pltpu.SemaphoreType.DMA
    attended, handed = pl.pallas_call(
        kernel,
        out_shape=(
            jax.ShapeDtypeStruct((1, ROWS, 512), BF16),
            jax.ShapeDtypeStruct((2 * FIN, PAGE, 2 * KVW), BF16),
        ),
        in_specs=[anywhere] * 4 + [whole] * 3 + [scalars] * 3,
        out_specs=(whole, anywhere),
        scratch_shapes=[
            pltpu.VMEM((ROWS, HEADS * HD), BF16),
            pltpu.VMEM((PAGES, PAGE, 2 * KVW), BF16),
            pltpu.VMEM((ROWS, 512), BF16),
            pltpu.VMEM((512, 2 * KVW), BF16),
            pltpu.VMEM((CTX, 2 * HD), BF16),
            pltpu.VMEM((CTX, 2 * HD), BF16),
            pltpu.VMEM((HD, CTX), BF16),
            pltpu.VMEM((BLOCKS, CTX, WIDE), F32),
            pltpu.VMEM((BLOCKS, CTX, WIDE), BF16),
            pltpu.VMEM((CTX + ROWS, HD), F32),
            pltpu.VMEM((CTX + ROWS, HD), F32),
            pltpu.VMEM((NX, 2, HD, CTX), BF16),
            pltpu.VMEM((NX, 4, CTX), F32),
            pltpu.VMEM((NX, 2, HD, CTX), BF16),
            pltpu.VMEM((NX, 4, CTX), F32),
            pltpu.VMEM((NX, HD, 512), BF16),
            pltpu.VMEM((NX, 2, 512), F32),
            pltpu.VMEM((NX, HD, 512), BF16),
            pltpu.VMEM((NX, 2, 512), F32),
            pltpu.VMEM((NX, 2, ROWS, 2 * HD), F32),
            pltpu.VMEM((NX, 2, ROWS, 2 * HD), F32),
            pltpu.VMEM((2, 2, ROWS, HD), F32),
            pltpu.VMEM((NX, 2, ROWS, HD), F32),
            pltpu.VMEM((PARTS, FIN, PAGE, PCOLS), BF16),
            pltpu.VMEM((PARTS, FIN, PAGE, PCOLS), BF16),
            pltpu.VMEM((FIN + 1, PAGE, PCOLS), BF16),
            pltpu.VMEM((PARTS, RANKS * CAP, PAGE, PCOLS), BF16),
            pltpu.VMEM((8, 128), jnp.int32),
            pltpu.VMEM((8, 128), jnp.int32),
            pltpu.SMEM((8, 128), jnp.int32),
            dma((4,)),
            dma,
            dma,
            dma,
            dma((PARTS,)),
            dma((PARTS,)),
        ]
        + [dma((NX,))] * 12
        + [dma((PARTS, RANKS)), dma((PARTS, RANKS)), dma((PARTS,))],
        compiler_params=pltpu.CompilerParams(
            collective_id=0, has_side_effects=True, vmem_limit_bytes=56 * 1024 * 1024
        ),
        cost_estimate=pl.CostEstimate(flops=4_500_000_000, bytes_accessed=12_000_000, transcendentals=8_500_000),
        name="attend_and_hand",
    )(
        queries[0],
        kv_cache.reshape(PAGES, PAGE, 2 * KVW),
        fresh_input[0],
        kv_weight,
        key_scale.reshape(1, KVW),
        cosine,
        sine,
        lengths.reshape(1),
        page_list,
        owners.reshape(FIN),
    )
    return pl.pallas_call(
        place_kernel,
        out_shape=(
            jax.ShapeDtypeStruct((1, ROWS, 512), BF16),
            jax.ShapeDtypeStruct((1, 2 * FIN, PAGE, 2 * KVW), BF16),
        ),
        in_specs=[whole] * 2,
        out_specs=(whole, whole),

        cost_estimate=pl.CostEstimate(flops=0, bytes_accessed=4_500_000, transcendentals=0),
        name="place",
    )(attended, handed)


def solution(mesh):
    return jax.shard_map(
        shards,
        mesh=mesh,
        in_specs=(
            P(("sec", "grp"), None, None),
            P(("sec", "grp"), "rank", None),
            P(),
            P(("sec", "grp"), None, "rank"),
            P("rank", None),
            P(("sec", "grp"), None),
            P(("sec", "grp", "rank")),
            P(("sec", "grp", "rank"), None),
        ),
        out_specs=(P(("sec", "grp"), None, "rank"), P(("sec", "grp", "rank"), None, None, None)),
        check_vma=False,
    )
```

```python
import functools
import math

import jax
import jax.numpy as jnp
from jax import lax
from jax.experimental import pallas as pl
from jax.experimental.pallas import tpu as pltpu
from jax.sharding import PartitionSpec as P

HEADS = 64
KVH = 8
HD = 128
ROWS = 128
CTX = 1024
PAGE = 16
GQ = 8
KVW = 1024
PAGES = CTX // PAGE
FIN = 16
CAP = 2
NX = 4
RANKS = NX * NX
TABLE = CTX + ROWS
PARTS = 8
PCOLS = 2 * KVW // PARTS
WINDOW = 2
UNITS = KVH
WIDE = 512
SPAN = 64
BLOCKS = GQ * ROWS // WIDE
SEND_AT = ((1, 2), (2, 3), (4, 4), (5, 5), (6, 6), (7, 7))
DISPATCH_AT = ((1,0),(3,1),(5,2),(7,3))
FRESH_AT = 6

ROPE_BASE = 500000.0
NEG_FILL = -1e30
TO_LOG2 = math.log2(math.e) / math.sqrt(HD)

F32 = jnp.float32
BF16 = jnp.bfloat16
MESH = pl.DeviceIdType.MESH


def rope_tables(positions):
    half_width = HD // 2
    steps_index = jnp.arange(half_width, dtype=jnp.float32)
    inverse = jnp.exp(steps_index * (-2.0 * math.log(ROPE_BASE) / HD))
    angles = positions.astype(jnp.float32) * jnp.concatenate([inverse, inverse])[None, :]
    return jnp.cos(angles), jnp.sin(angles)


def rotate(values, cosine, sine):
    swapped = pltpu.roll(values, HD // 2, 1)
    return values * cosine + swapped * sine


def dot_nt(a, b):
    return lax.dot_general(a, b, (((1,), (1,)), ((), ())), preferred_element_type=F32)


def soft_block(scores):
    peak = jnp.max(scores, axis=0, keepdims=True)
    weights = jnp.exp2(scores * TO_LOG2 - peak * TO_LOG2)
    total = jnp.sum(weights, axis=0, keepdims=True)
    return peak * TO_LOG2, total, weights.astype(BF16)


def merge(parts):
    top = functools.reduce(jnp.maximum, [p[0] for p in parts])
    factors = [jnp.exp2(p[0] - top) for p in parts]
    total = sum(p[1] * f for p, f in zip(parts, factors))
    numerator = sum(p[2] * f for p, f in zip(parts, factors))
    return top, total, numerator


def kernel(
    q_hbm, cache_hbm, fin_hbm, w_hbm, scale_ref, cos_half, sin_half, len_ref, plist_ref, own_ref,
    att_ref, handed_ref,
    q_ref, cache_ref, fin_ref, w_ref,
    keys, rows, vals_t, scores, weights, cos_ref, sin_ref,
    xs, xst, xr, xrt, zs, zst, zr, zrt,
    fs, fr, gs, gr,
    page_out, landed, work, picked, meta_out, meta_in, meta,
    load_sem, meta_send, meta_recv, meta_load, page_send, page_recv,
    xs_send, xs_recv, xt_send, xt_recv, zs_send, zs_recv, zt_send, zt_recv,
    f_send, f_recv, g_send, g_recv, pick_send, pick_recv, own_sem,
):
    sec, grp, rank = lax.axis_index("sec"), lax.axis_index("grp"), lax.axis_index("rank")
    x, z = lax.div(rank, NX), lax.rem(rank, NX)

    def at(xx, zz, section=None):
        return (sec if section is None else section, grp, xx * NX + zz)

    def remote(src, dst, send, recv, device):
        return pltpu.make_async_remote_copy(
            src_ref=src, dst_ref=dst, send_sem=send, recv_sem=recv, device_id=device, device_id_type=MESH
        )

    def plus(value, by):
        return lax.rem(value + by, NX)

    loads = [
        pltpu.make_async_copy(src, dst, load_sem.at[i])
        for i, (src, dst) in enumerate(
            ((cache_hbm, cache_ref), (fin_hbm, fin_ref), (w_hbm, w_ref), (q_hbm, q_ref))
        )
    ]
    for load in loads:
        load.start()

    barrier = pltpu.get_barrier_semaphore()
    for o in range(1, RANKS):
        peer = lax.rem(rank + o, RANKS)
        pl.semaphore_signal(barrier, inc=1, device_id=(sec, grp, peer), device_id_type=MESH)
    pl.semaphore_signal(barrier, inc=1, device_id=at(x, NX - 1 - z, 1 - sec), device_id_type=MESH)

    def page_copy(part):
        return remote(
            page_out.at[part], landed.at[part], page_send.at[part], page_recv.at[part], at(x, NX - 1 - z, 1)
        )

    def meta_copy():
        return remote(meta_out, meta_in, meta_send, meta_recv, at(x, NX - 1 - z, 1))

    loads[0].wait()

    @pl.when(sec == 0)
    def _():
        lanes = lax.broadcasted_iota(jnp.int32, (8, 128), 1)
        owner_of, slot_of = lanes // CAP, lanes % CAP
        count = jnp.zeros((8, 128), jnp.int32)
        chosen = jnp.full((8, 128), FIN, jnp.int32)
        for f in range(FIN):
            mine = owner_of == own_ref[f]
            chosen = jnp.where(mine & (count == slot_of), f, chosen)
            count = count + jnp.where(mine, 1, 0)
        meta_out[...] = chosen

        @pl.loop(0, FIN)
        def _(f):
            page = plist_ref[f]
            for part in range(PARTS):
                page_out[part, f] = cache_ref[page, :, part * PCOLS : (part + 1) * PCOLS]

    loads[1].wait()
    loads[2].wait()

    def fresh_x(xx):
        o = plus(xx - x + NX, 0)
        return remote(fs.at[xx], fr.at[o], f_send.at[o], f_recv.at[o], at(xx, z))

    for xx in range(NX):
        for kind in range(2):
            cols = slice(kind * KVW + xx * 2 * HD, kind * KVW + (xx + 1) * 2 * HD)
            fs[xx, kind] = jnp.dot(fin_ref[...], w_ref[:, cols], preferred_element_type=F32)

    low = lax.broadcasted_iota(jnp.int32, (TABLE // 2, HD), 1) < HD // 2
    cosine, sine = cos_half[...], sin_half[...]
    cosine_swapped, sine_swapped = pltpu.roll(cosine, HD // 2, 1), pltpu.roll(sine, HD // 2, 1)
    cos_ref[: TABLE // 2] = jnp.where(low, cosine, cosine_swapped)
    cos_ref[TABLE // 2 :] = jnp.where(low, cosine_swapped, cosine)
    sin_ref[: TABLE // 2] = jnp.where(low, -sine, sine_swapped)
    sin_ref[TABLE // 2 :] = jnp.where(low, -sine_swapped, sine)
    loads[3].wait()
    pl.semaphore_wait(barrier, RANKS)

    @pl.when(sec == 0)
    def _():
        meta_copy().start()
        for part in range(WINDOW):
            page_copy(part).start()

    for xx in range(NX):

        @pl.when(xx != x)
        def _():
            fresh_x(xx).start()

    def fresh_z(zz):
        o = plus(zz - z + NX, 0)
        return remote(gs.at[zz // 2], gr.at[o], g_send.at[o], g_recv.at[o], at(x, zz))

    def fresh_sum_x():
        for o in range(1, NX):
            remote(fs.at[0], fr.at[o], f_send.at[o], f_recv.at[o], at(plus(x, o), z)).wait_recv()
        for kind in range(2):
            total = fs[x, kind] + fr[1, kind] + fr[2, kind] + fr[3, kind]
            gs[0, kind] = total[:, :HD]
            gs[1, kind] = total[:, HD:]
        for zz in range(NX):

            @pl.when(zz != z)
            def _():
                fresh_z(zz).start()

    source = x * NX + NX - 1 - z

    def picked_copy(part, o):
        owner = lax.rem(rank + o, RANKS)
        return remote(
            picked.at[part, pl.ds(owner * CAP, CAP)],
            handed_ref.at[pl.ds(source * CAP, CAP), :, pl.ds(part * PCOLS, PCOLS)],
            pick_send.at[part, o],
            pick_recv.at[part, o],
            (1, grp, owner),
        )

    def picked_own(part):
        return pltpu.make_async_copy(
            picked.at[part, pl.ds(rank * CAP, CAP)],
            handed_ref.at[pl.ds(source * CAP, CAP), :, pl.ds(part * PCOLS, PCOLS)],
            own_sem.at[part],
        )

    def dispatch(part):
        if part == 0:
            meta_copy().wait_recv()
            load = pltpu.make_async_copy(meta_in, meta, meta_load)
            load.start()
            load.wait()
        page_copy(part).wait_recv()
        work[:FIN] = landed[part]
        for owner in range(RANKS):
            for c in range(CAP):
                picked[part, owner * CAP + c] = work[meta[0, owner * CAP + c]]

        @pl.loop(1, RANKS)
        def _(o):
            picked_copy(part, o).start()

        picked_own(part).start()

    def in_decode(*parts):
        @pl.when(sec == 1)
        def _():
            for part in parts:
                dispatch(part)

    @pl.when(sec == 1)
    def _():
        work[FIN] = jnp.zeros((PAGE, PCOLS), BF16)

    edge = len_ref[0] - rank * CTX
    inside = lax.broadcasted_iota(jnp.int32, (CTX, HD), 0) < edge
    first = lax.broadcasted_iota(jnp.int32, (CTX, HD), 1) == 0
    keys[:, HD:] = jnp.where(first & jnp.logical_not(inside), NEG_FILL, 0.0).astype(BF16)
    rows[:, HD:] = jnp.where(first, 1.0, 0.0).astype(BF16)

    def head_copy(o, h):
        xx = plus(x, o)
        return remote(xs.at[xx, h], xr.at[o, h], xs_send.at[o, h], xs_recv.at[o, h], at(xx, z))

    def stat_copy(o):
        xx = plus(x, o)
        return remote(xst.at[xx], xrt.at[o], xt_send.at[o], xt_recv.at[o], at(xx, z))

    def xs_copy(o):
        return head_copy(o, 0), head_copy(o, 1), stat_copy(o)

    @pl.loop(0, UNITS)
    def _(u):
        o = plus(lax.div(u, 2), 1)
        xx, hh = plus(x, o), lax.rem(u, 2)
        head = xx * 2 + hh
        cols = pl.ds(pl.multiple_of(head * HD, HD), HD)
        val_cols = pl.ds(pl.multiple_of(KVW + head * HD, HD), HD)
        for c in range(CTX // 128):
            span, pages = slice(c * 128, (c + 1) * 128), slice(c * 8, (c + 1) * 8)
            raw = cache_ref[pages, :, cols].reshape(128, HD).astype(F32) * scale_ref[:, cols]
            keys[span, :HD] = rotate(raw, cos_ref[span, :], sin_ref[span, :]).astype(BF16)
            vals_t[:, span] = cache_ref[pages, :, val_cols].reshape(128, HD).T
        for g in range(GQ):
            q_cols = pl.ds(pl.multiple_of((head * GQ + g) * HD, HD), HD)
            rows[g * ROWS : (g + 1) * ROWS, :HD] = rotate(
                q_ref[:, q_cols].astype(F32), cos_ref[CTX:, :], sin_ref[CTX:, :]
            ).astype(BF16)

        def score(b):
            scores[b] = dot_nt(keys[...], rows[b * WIDE : (b + 1) * WIDE, :])

        def weigh(b):
            peaks = scores[b, :SPAN].reshape(SPAN // 8, 8, WIDE).max(axis=0)
            for c in range(1, CTX // SPAN):
                part = scores[b, c * SPAN : (c + 1) * SPAN].reshape(SPAN // 8, 8, WIDE)
                peaks = jnp.maximum(peaks, part.max(axis=0))
            peak = peaks.max(axis=0, keepdims=True) * TO_LOG2
            base = jnp.broadcast_to(peak, (8, WIDE))
            totals = jnp.zeros((8, WIDE), F32)
            for c in range(CTX // SPAN):
                part = scores[b, c * SPAN : (c + 1) * SPAN].reshape(SPAN // 8, 8, WIDE)
                grown = jnp.exp2(part * TO_LOG2 - base[None])
                totals = totals + grown.sum(axis=0)
                weights[b, c * SPAN : (c + 1) * SPAN] = grown.reshape(SPAN, WIDE).astype(BF16)
            return peak, totals.sum(axis=0, keepdims=True)

        def add_up(b):
            numerator = jnp.dot(vals_t[...], weights[b], preferred_element_type=F32)
            xs[xx, hh, :, b * WIDE : (b + 1) * WIDE] = numerator.astype(BF16)

        stats = []
        score(0)
        for b in range(BLOCKS):
            if b + 1 < BLOCKS:
                score(b + 1)
            if b > 0:
                add_up(b - 1)
            stats.append(weigh(b))
        add_up(BLOCKS - 1)
        for h in range(2):

            @pl.when(hh == h)
            def _():
                for b in range(BLOCKS):
                    for i in range(2):
                        row = 2 * h + i
                        xst[xx, row : row + 1, b * WIDE : (b + 1) * WIDE] = stats[b][i]

        @pl.when(o != 0)
        def _():
            head_copy(o, hh).start()

        @pl.when((hh == 1) & (o != 0))
        def _():
            stat_copy(o).start()

        for unit, part in SEND_AT:

            @pl.when((sec == 0) & (u == unit))
            def _():
                page_copy(part - WINDOW).wait_send()
                page_copy(part).start()

        for unit, part in DISPATCH_AT:

            @pl.when((sec == 1) & (u == unit))
            def _():
                dispatch(part)

        @pl.when(u == FRESH_AT)
        def _():
            fresh_sum_x()

    @pl.when(sec == 0)
    def _():
        picked[0] = jnp.zeros((RANKS * CAP, PAGE, PCOLS), BF16)
        for part in range(PARTS):
            pltpu.make_async_copy(
                picked.at[0], handed_ref.at[:, :, pl.ds(part * PCOLS, PCOLS)], own_sem.at[part]
            ).start()

    in_decode(4, 5, 6, 7)

    for o in range(1, NX):
        for copy in xs_copy(o):
            copy.wait_recv()

    def zs_copy(zz):
        o = plus(zz - z + NX, 0)
        return (
            remote(zs.at[zz], zr.at[o], zs_send.at[o], zs_recv.at[o], at(x, zz)),
            remote(zst.at[zz], zrt.at[o], zt_send.at[o], zt_recv.at[o], at(x, zz)),
        )

    for zz in range(NX):
        hh, cols = zz // 2, slice((zz % 2) * 512, (zz % 2 + 1) * 512)
        parts = [
            (xst[x, 2 * hh : 2 * hh + 1, cols], xst[x, 2 * hh + 1 : 2 * hh + 2, cols], xs[x, hh, :, cols].astype(F32))
        ]
        for o in range(1, NX):
            parts.append(
                (
                    xrt[o, 2 * hh : 2 * hh + 1, cols],
                    xrt[o, 2 * hh + 1 : 2 * hh + 2, cols],
                    xr[o, hh, :, cols].astype(F32),
                )
            )
        top, total, numerator = merge(parts)
        zs[zz] = numerator.astype(BF16)
        zst[zz, 0:1, :] = top
        zst[zz, 1:2, :] = total

        @pl.when(zz != z)
        def _():
            for copy in zs_copy(zz):
                copy.start()


    for o in range(1, NX):
        remote(gs.at[0], gr.at[o], g_send.at[o], g_recv.at[o], at(x, plus(z, o))).wait_recv()
    mine = lax.div(z, 2)
    fresh = [(gs[mine, kind] + gr[1, kind] + gr[2, kind] + gr[3, kind]).astype(BF16) for kind in range(2)]
    fresh_keys = rotate(fresh[0].astype(F32), cos_ref[CTX:, :], sin_ref[CTX:, :]).astype(BF16)
    own_rows = []
    for h in range(HEADS // (NX * NX)):
        q_cols = pl.ds(pl.multiple_of((rank * 4 + h) * HD, HD), HD)
        own_rows.append(rotate(q_ref[:, q_cols].astype(F32), cos_ref[CTX:, :], sin_ref[CTX:, :]).astype(BF16))
    fresh_scores = dot_nt(fresh_keys, jnp.concatenate(own_rows, axis=0))
    key_row = lax.broadcasted_iota(jnp.int32, fresh_scores.shape, 0)
    query_row = lax.broadcasted_iota(jnp.int32, fresh_scores.shape, 1) % ROWS
    peak, total, fresh_weights = soft_block(jnp.where(key_row <= query_row, fresh_scores, NEG_FILL))
    numerator = jnp.dot(fresh[1].astype(F32).T.astype(BF16), fresh_weights, preferred_element_type=F32)
    parts = [(peak, total, numerator)]

    for o in range(1, NX):
        for copy in zs_copy(plus(z, o)):
            copy.wait_recv()
    parts.append((zst[z, 0:1, :], zst[z, 1:2, :], zs[z].astype(F32)))
    for o in range(1, NX):
        parts.append((zrt[o, 0:1, :], zrt[o, 1:2, :], zr[o].astype(F32)))
    _, total, numerator = merge(parts)
    result = numerator / total
    for h in range(HEADS // (NX * NX)):
        att_ref[0, :, h * HD : (h + 1) * HD] = result[:, h * ROWS : (h + 1) * ROWS].T.astype(BF16)

    for o in range(1, NX):
        for copy in xs_copy(o):
            copy.wait_send()
        for copy in zs_copy(plus(z, o)):
            copy.wait_send()
        fresh_x(plus(x, o)).wait_send()
        remote(gs.at[0], gr.at[o], g_send.at[o], g_recv.at[o], at(x, plus(z, o))).wait_send()

    @pl.when(sec == 0)
    def _():
        meta_copy().wait_send()
        for part in range(PARTS - WINDOW, PARTS):
            page_copy(part).wait_send()
        for part in range(PARTS):
            pltpu.make_async_copy(
                picked.at[0], handed_ref.at[:, :, pl.ds(part * PCOLS, PCOLS)], own_sem.at[part]
            ).wait()

    @pl.when(sec == 1)
    def _():
        for part in range(PARTS):

            @pl.loop(1, RANKS)
            def _(o):
                picked_copy(part, o).wait_send()
                picked_copy(part, o).wait_recv()

            picked_own(part).wait()


def place_kernel(att_in, handed_in, att_out, handed_out):
    att_out[...] = att_in[...]
    handed_out[0] = handed_in[...]


def shards(queries, kv_cache, key_scale, fresh_input, kv_weight, lengths, page_list, owners):
    position = lax.axis_index("rank")
    length = lengths[0, 0]
    places = lax.broadcasted_iota(jnp.int32, (TABLE // 2, HD), 0)
    lanes = lax.broadcasted_iota(jnp.int32, (TABLE // 2, HD), 1)
    places = places + jnp.where(lanes < HD // 2, 0, TABLE // 2)
    cosine, sine = rope_tables(jnp.where(places < CTX, position * CTX, length - CTX) + places)
    whole = pl.BlockSpec(memory_space=pltpu.VMEM)
    scalars = pl.BlockSpec(memory_space=pltpu.SMEM)
    anywhere = pl.BlockSpec(memory_space=pl.ANY)
    dma = pltpu.SemaphoreType.DMA
    attended, handed = pl.pallas_call(
        kernel,
        out_shape=(
            jax.ShapeDtypeStruct((1, ROWS, 512), BF16),
            jax.ShapeDtypeStruct((2 * FIN, PAGE, 2 * KVW), BF16),
        ),
        in_specs=[anywhere] * 4 + [whole] * 3 + [scalars] * 3,
        out_specs=(whole, anywhere),
        scratch_shapes=[
            pltpu.VMEM((ROWS, HEADS * HD), BF16),
            pltpu.VMEM((PAGES, PAGE, 2 * KVW), BF16),
            pltpu.VMEM((ROWS, 512), BF16),
            pltpu.VMEM((512, 2 * KVW), BF16),
            pltpu.VMEM((CTX, 2 * HD), BF16),
            pltpu.VMEM((CTX, 2 * HD), BF16),
            pltpu.VMEM((HD, CTX), BF16),
            pltpu.VMEM((BLOCKS, CTX, WIDE), F32),
            pltpu.VMEM((BLOCKS, CTX, WIDE), BF16),
            pltpu.VMEM((CTX + ROWS, HD), F32),
            pltpu.VMEM((CTX + ROWS, HD), F32),
            pltpu.VMEM((NX, 2, HD, CTX), BF16),
            pltpu.VMEM((NX, 4, CTX), F32),
            pltpu.VMEM((NX, 2, HD, CTX), BF16),
            pltpu.VMEM((NX, 4, CTX), F32),
            pltpu.VMEM((NX, HD, 512), BF16),
            pltpu.VMEM((NX, 2, 512), F32),
            pltpu.VMEM((NX, HD, 512), BF16),
            pltpu.VMEM((NX, 2, 512), F32),
            pltpu.VMEM((NX, 2, ROWS, 2 * HD), F32),
            pltpu.VMEM((NX, 2, ROWS, 2 * HD), F32),
            pltpu.VMEM((2, 2, ROWS, HD), F32),
            pltpu.VMEM((NX, 2, ROWS, HD), F32),
            pltpu.VMEM((PARTS, FIN, PAGE, PCOLS), BF16),
            pltpu.VMEM((PARTS, FIN, PAGE, PCOLS), BF16),
            pltpu.VMEM((FIN + 1, PAGE, PCOLS), BF16),
            pltpu.VMEM((PARTS, RANKS * CAP, PAGE, PCOLS), BF16),
            pltpu.VMEM((8, 128), jnp.int32),
            pltpu.VMEM((8, 128), jnp.int32),
            pltpu.SMEM((8, 128), jnp.int32),
            dma((4,)),
            dma,
            dma,
            dma,
            dma((PARTS,)),
            dma((PARTS,)),
        ]
        + [dma((NX, 2))] * 2
        + [dma((NX,))] * 10
        + [dma((PARTS, RANKS)), dma((PARTS, RANKS)), dma((PARTS,))],
        compiler_params=pltpu.CompilerParams(
            collective_id=0, has_side_effects=True, vmem_limit_bytes=56 * 1024 * 1024
        ),
        cost_estimate=pl.CostEstimate(flops=4_500_000_000, bytes_accessed=12_000_000, transcendentals=8_500_000),
        name="attend_and_hand",
    )(
        queries[0],
        kv_cache.reshape(PAGES, PAGE, 2 * KVW),
        fresh_input[0],
        kv_weight,
        key_scale.reshape(1, KVW),
        cosine,
        sine,
        lengths.reshape(1),
        page_list,
        owners.reshape(FIN),
    )
    return pl.pallas_call(
        place_kernel,
        out_shape=(
            jax.ShapeDtypeStruct((1, ROWS, 512), BF16),
            jax.ShapeDtypeStruct((1, 2 * FIN, PAGE, 2 * KVW), BF16),
        ),
        in_specs=[whole] * 2,
        out_specs=(whole, whole),

        cost_estimate=pl.CostEstimate(flops=0, bytes_accessed=4_500_000, transcendentals=0),
        name="place",
    )(attended, handed)


def solution(mesh):
    return jax.shard_map(
        shards,
        mesh=mesh,
        in_specs=(
            P(("sec", "grp"), None, None),
            P(("sec", "grp"), "rank", None),
            P(),
            P(("sec", "grp"), None, "rank"),
            P("rank", None),
            P(("sec", "grp"), None),
            P(("sec", "grp", "rank")),
            P(("sec", "grp", "rank"), None),
        ),
        out_specs=(P(("sec", "grp"), None, "rank"), P(("sec", "grp", "rank"), None, None, None)),
        check_vma=False,
    )
```
